256 devices in a mesh: blk: 64 (over y_hi, z, x), head: 4 (over y_lo, core).
Axes of the slice: x: 4, y: 4 (y_hi: 2, y_lo: 2; y = y_hi * 2 + y_lo), z: 8, core: 2. Of those that a mesh axis runs over, the one named last changes fastest.
Arguments:
- queries: bfloat16 [32768, 1024], P(('blk', 'head')), may hold values from -5.25 to 5.25
- keys: bfloat16 [32768, 1024], P(('blk', 'head')), may hold values from -5.25 to 5.25
- values: bfloat16 [32768, 1024], P(('blk', 'head')), may hold values from -5 to 5
- out_grad: bfloat16 [32768, 1024], P(('blk', 'head')), may hold values from -5 to 5
- node_order: int32 [32768], P('blk'), may hold values from 0 to 511, as said below
- block_lists: int32 [256, 12], P('blk'), may hold values from 0 to 19, as said below
- block_counts: int32 [256], P('blk'), may hold values from 1 to 12
Outputs:
- attn_out: bfloat16 [32768, 1024], P(('blk', 'head'))
- query_grad: bfloat16 [32768, 1024], P(('blk', 'head'))
- key_grad: bfloat16 [32768, 1024], P(('blk', 'head'))
- value_grad: bfloat16 [32768, 1024], P(('blk', 'head'))
The draws below stay inside these ranges and needn't reach their ends.
Inputs may be any that keep to these rules, and one draw needn't show every extreme that they name: `node_order`: within each aligned block of 512 entries, every number of 0 to 511 stands once. `block_lists`: the entries of a row are distinct; the first is the block's own entry 8 + g % 4.
All inputs are finite; a program needn't handle non-finite values.
Results may differ from the reference program's by a relative error of at most 0.035.
Values may be sent and summed in bfloat16 or wider, within the bound.
A program may use at most 192 MiB of HBM per device.

```python
import math
import jax
import jax.numpy as jnp
from jax import lax

HEADS = 16
HEAD_DIM = 64
D = 1024
BLOCK = 128
LIST = 12
BLOCKS_DEV = 4
NBLOCKS = 256
NODES = 32768


def order_table(key):
    segments = NBLOCKS // BLOCKS_DEV
    seg_keys = jax.random.split(key, segments)
    return jax.vmap(lambda subkey: jax.random.permutation(subkey, BLOCKS_DEV * BLOCK))(seg_keys).astype(jnp.int32)


def draw_node_order(key, part):
    return order_table(key).reshape(-1)


def draw_queries(key, part):
    key = jax.random.fold_in(key, 3)
    return jnp.clip(jax.random.normal(key, (NODES, D), jnp.float32), -5.0, 5.0).astype(jnp.bfloat16)


def draw_keys(key, part):
    key = jax.random.fold_in(key, 5)
    return jnp.clip(jax.random.normal(key, (NODES, D), jnp.float32), -5.0, 5.0).astype(jnp.bfloat16)


def draw_block_lists(key, part):
    key = jax.random.fold_in(key, 7)
    candidates = 5 * BLOCKS_DEV
    block_ids = jnp.arange(NBLOCKS, dtype=jnp.int32)
    column = jnp.arange(candidates, dtype=jnp.int32)
    noise_int = jax.random.randint(key, (NBLOCKS, candidates), 0, 65536, dtype=jnp.int32)
    scores = noise_int * 512 + column[None, :]
    is_own = column[None, :] == 2 * BLOCKS_DEV + (block_ids % BLOCKS_DEV)[:, None]
    is_edge = (block_ids[:, None] == 0) & ((column[None, :] == 0) | (column[None, :] == candidates - 1))
    scores = scores + is_own.astype(jnp.int32) * 2 ** 26 + is_edge.astype(jnp.int32) * 2 ** 25
    ranked, chosen = lax.top_k(scores, LIST)
    return chosen.astype(jnp.int32)


def draw_block_counts(key, part):
    key = jax.random.fold_in(key, 9)
    level_key, count_key = jax.random.split(key)
    segments = NBLOCKS // BLOCKS_DEV
    weight = jax.random.randint(level_key, (segments,), 1, 5, dtype=jnp.int32)
    ceiling = jnp.repeat(weight * LIST // 4, BLOCKS_DEV)
    counts = jax.random.randint(count_key, (NBLOCKS,), 1, ceiling + 1, dtype=jnp.int32)
    return counts.at[0].set(LIST)


def shard_levels(stream_key, shape, cuts, least, largest):
    gain = 1.0
    for axis_at, blocks in cuts:
        draws = jax.random.uniform(jax.random.fold_in(jax.random.fold_in(stream_key, 6), axis_at), (blocks,), jnp.float32, least / len(cuts), largest / len(cuts))
        gain = gain * jnp.repeat(jnp.exp(draws), shape[axis_at] // blocks).reshape((-1,) + (1,) * (len(shape) - 1 - axis_at))
    return gain


def noise(key, shape, width, most, cuts=(), kind=jnp.bfloat16):
    loudness = shard_levels(key, shape, cuts, -0.22, 0.18) if cuts else 1.0
    values = jax.random.normal(key, shape, jnp.float32) * width * loudness
    return jnp.minimum(jnp.maximum(values, -most), most).astype(kind)


def setup_inputs(seed: int = 0) -> dict:
    key_list = jax.random.split(jax.random.key(seed), 8)
    return {
        "queries": draw_queries(jax.random.fold_in(key_list[7], 71), 0),
        "keys": draw_keys(jax.random.fold_in(key_list[7], 71), 0),
        "values": noise(key_list[2], (NODES, D), 1.0, 5.0, ((0, 256),)),
        "out_grad": noise(key_list[3], (NODES, D), 1.0, 5.0, ((0, 256),)),
        "node_order": draw_node_order(jax.random.fold_in(key_list[7], 71), 0),
        "block_lists": draw_block_lists(jax.random.fold_in(key_list[7], 71), 0),
        "block_counts": draw_block_counts(jax.random.fold_in(key_list[7], 71), 0),
    }


def reference(queries, keys, values, out_grad, node_order, block_lists, block_counts):
    seg_rows = BLOCKS_DEV * BLOCK
    segments = NBLOCKS // BLOCKS_DEV
    key_span = LIST * BLOCK
    score_scale = 1.0 / math.sqrt(HEAD_DIM)
    blocked_order = (jnp.arange(segments, dtype=jnp.int32)[:, None] * seg_rows + node_order.reshape(segments, seg_rows)).reshape(-1)
    q_p = queries[blocked_order]
    k_p = keys[blocked_order]
    v_p = values[blocked_order]
    g_p = out_grad[blocked_order]
    slot_of = jnp.arange(key_span, dtype=jnp.int32) // BLOCK

    def one_block(totals, block_index):
        key_sum, value_sum = totals
        segment = block_index // BLOCKS_DEV
        entries = block_lists[block_index]
        target = (segment + entries // BLOCKS_DEV - 2) % segments * BLOCKS_DEV + entries % BLOCKS_DEV
        key_index = (target[:, None] * BLOCK + jnp.arange(BLOCK, dtype=jnp.int32)[None, :]).reshape(-1)
        first_row = block_index * BLOCK
        query_rows = lax.dynamic_slice_in_dim(q_p, first_row, BLOCK, 0).astype(jnp.float32).reshape(BLOCK, HEADS, HEAD_DIM)
        grad_rows = lax.dynamic_slice_in_dim(g_p, first_row, BLOCK, 0).astype(jnp.float32).reshape(BLOCK, HEADS, HEAD_DIM)
        key_rows = k_p[key_index].astype(jnp.float32).reshape(key_span, HEADS, HEAD_DIM)
        value_rows = v_p[key_index].astype(jnp.float32).reshape(key_span, HEADS, HEAD_DIM)
        is_live = slot_of < block_counts[block_index]
        scores = jnp.einsum('qhd,khd->hqk', query_rows, key_rows) * score_scale
        scores = jnp.where(is_live[None, None, :], scores, -jnp.inf)
        row_max = lax.optimization_barrier(jnp.max(scores, axis=-1, keepdims=True))
        shifted = jnp.exp(scores - row_max)
        chance = shifted / lax.optimization_barrier(jnp.sum(shifted, axis=-1, keepdims=True))
        chance_low = lax.optimization_barrier(chance.astype(jnp.bfloat16)).astype(jnp.float32)
        attended = jnp.einsum('hqk,khd->qhd', chance_low, value_rows).astype(jnp.bfloat16)
        attended_f = lax.optimization_barrier(attended).astype(jnp.float32)
        inner_dot = jnp.einsum('qhd,qhd->hq', grad_rows, attended_f)
        grad_chance = jnp.einsum('qhd,khd->hqk', grad_rows, value_rows)
        grad_score = chance * (grad_chance - inner_dot[:, :, None])
        grad_low = lax.optimization_barrier(grad_score.astype(jnp.bfloat16)).astype(jnp.float32)
        query_part = (jnp.einsum('hqk,khd->qhd', grad_low, key_rows) * score_scale).astype(jnp.bfloat16)
        key_part = jnp.einsum('hqk,qhd->khd', grad_low, query_rows).reshape(key_span, D)
        value_part = jnp.einsum('hqk,qhd->khd', chance_low, grad_rows).reshape(key_span, D)
        key_sum = key_sum.at[key_index].add(key_part)
        value_sum = value_sum.at[key_index].add(value_part)
        return ((key_sum, value_sum), (attended.reshape(BLOCK, D), query_part.reshape(BLOCK, D)))
    empty_sum = jnp.zeros((NODES, D), jnp.float32)
    (key_sum, value_sum), (attended, query_part) = lax.scan(one_block, (empty_sum, empty_sum), jnp.arange(NBLOCKS, dtype=jnp.int32))
    key_low = (key_sum * score_scale).astype(jnp.bfloat16)
    value_low = value_sum.astype(jnp.bfloat16)
    blank = jnp.zeros((NODES, D), jnp.bfloat16)
    attn_out = blank.at[blocked_order].set(attended.reshape(NODES, D))
    query_grad = blank.at[blocked_order].set(query_part.reshape(NODES, D))
    key_grad = blank.at[blocked_order].set(key_low)
    value_grad = blank.at[blocked_order].set(value_low)
    return (attn_out, query_grad, key_grad, value_grad)
```

```python
import functools
import math

import jax
import jax.numpy as jnp
from jax import lax
from jax.experimental import pallas as pl
from jax.experimental.pallas import tpu as pltpu
from jax.sharding import PartitionSpec as P

BLK = 128
SEG = 512
DIM = 64
LIST = 12
GROUP = 16
NT = (((1,), (1,)), ((), ()))
TN = (((0,), (0,)), ((), ()))
SCALE = 1.0 / math.sqrt(DIM)
LOG2E = math.log2(math.e)
MESH = pl.DeviceIdType.MESH
ANY = pl.BlockSpec(memory_space=pl.ANY)
VMEM = pl.BlockSpec(memory_space=pltpu.VMEM)
SMEM = pl.BlockSpec(memory_space=pltpu.SMEM)


def place():
    blk, head = lax.axis_index("blk"), lax.axis_index("head")
    segs = lax.axis_size("blk")
    quad = blk // 4
    me = (blk % 4) * 4 + head
    left = (lax.rem(blk + segs - 4, segs), head)
    right = (lax.rem(blk + 4, segs), head)
    return quad, me, left, right


def member(quad, slot):
    return (quad * 4 + slot // 4, slot % 4)


def remote(src, dst, ssem, rsem, device):
    return pltpu.make_async_remote_copy(
        src_ref=src, dst_ref=dst, send_sem=ssem, recv_sem=rsem, device_id=device, device_id_type=MESH
    )


def greet(quad, me, left, right):
    barrier = pltpu.get_barrier_semaphore()
    for step in range(1, GROUP):
        pl.semaphore_signal(
            barrier, inc=1, device_id=member(quad, lax.rem(me + step, GROUP)), device_id_type=MESH
        )
    for device in (left, right):
        pl.semaphore_signal(barrier, inc=1, device_id=device, device_id_type=MESH)
    pl.semaphore_wait(barrier, GROUP + 1)


def enter_kernel(
    q_ref, k_ref, v_ref, g_ref, order_ref, lists_ref, counts_ref,
    window_ref, qg_ref, orders_ref, meta_ref,
    kv_out, qg_out, kv_in, qg_in, own_kv, own_qg, order_in, meta_in,
    kv_ss, kv_rs, qg_ss, qg_rs, order_ss, order_rs, meta_ss, meta_rs, halo_ss, halo_rs, local_sem,
):
    quad, me, left, right = place()
    seg = me // 4
    head = me % 4
    meta_in[seg] = jnp.zeros((8, 128), jnp.int32)
    meta_in[seg, 0:4, 0:LIST] = lists_ref[...]
    meta_in[seg, 4:5, 0:4] = counts_ref[...]
    order_in[seg] = order_ref[...]
    for t in range(8):
        cols = slice(t * 128, t * 128 + 128)
        k, v = k_ref[:, cols], v_ref[:, cols]
        kv_out[2 * t] = jnp.concatenate([k[:, :DIM], v[:, :DIM]], axis=1)
        kv_out[2 * t + 1] = jnp.concatenate([k[:, DIM:], v[:, DIM:]], axis=1)
    greet(quad, me, left, right)
    small = []
    for step in range(1, 4):
        peer = member(quad, lax.rem(me + 4 * step, GROUP))
        small.append(remote(order_in.at[seg], order_in.at[seg], order_ss.at[step], order_rs.at[seg], peer))
        small.append(remote(meta_in.at[seg], meta_in.at[seg], meta_ss.at[step], meta_rs.at[seg], peer))
    for copy in small:
        copy.start()
    sends = []
    for step in range(1, GROUP):
        slot = lax.rem(me + step, GROUP)
        sends.append(
            remote(kv_out.at[slot], kv_in.at[me], kv_ss.at[step], kv_rs.at[me], member(quad, slot))
        )
        sends[-1].start()
    kv_in[me] = kv_out[me]
    for t in range(8):
        cols = slice(t * 128, t * 128 + 128)
        q, g = q_ref[:, cols] * SCALE, g_ref[:, cols]
        qg_out[2 * t] = jnp.concatenate([q[:, :DIM], g[:, :DIM]], axis=1)
        qg_out[2 * t + 1] = jnp.concatenate([q[:, DIM:], g[:, DIM:]], axis=1)
    for step in range(1, GROUP):
        slot = lax.rem(me + step, GROUP)
        sends.append(
            remote(qg_out.at[slot], qg_in.at[me], qg_ss.at[step], qg_rs.at[me], member(quad, slot))
        )
        sends[-1].start()
    qg_in[me] = qg_out[me]

    for s in range(4):

        @pl.when(s != seg)
        def _():
            remote(order_in.at[s], order_in.at[s], order_ss.at[0], order_rs.at[s], left).wait_recv()
            remote(meta_in.at[s], meta_in.at[s], meta_ss.at[0], meta_rs.at[s], left).wait_recv()

    def one_hot(s):
        order = jnp.broadcast_to(order_in[s].astype(jnp.float32), (128, SEG))
        order = jnp.transpose(order)
        lane = lax.broadcasted_iota(jnp.int32, (SEG, 128), 1).astype(jnp.float32)
        tiles = [(order == lane + 128.0 * t).astype(jnp.bfloat16) for t in range(4)]
        return jnp.concatenate(tiles, axis=1)

    picks = [one_hot(s) for s in range(4)]
    locals_ = [
        pltpu.make_async_copy(order_in, orders_ref, local_sem.at[8]),
        pltpu.make_async_copy(meta_in, meta_ref, local_sem.at[9]),
    ]
    for copy in locals_:
        copy.start()
    halos = []
    for s in range(4):
        for slot in range(4 * s, 4 * s + 4):

            @pl.when(slot != me)
            def _():
                remote(kv_in.at[slot], kv_in.at[slot], kv_ss.at[0], kv_rs.at[slot], left).wait_recv()

        rows = pl.ds(s * SEG, SEG)
        own_kv[rows, :] = jnp.dot(
            picks[s], kv_in[4 * s : 4 * s + 4].reshape(SEG, 128), preferred_element_type=jnp.float32
        ).astype(jnp.bfloat16)
        there = 3072 + s * SEG if s < 2 else (s - 2) * SEG
        halos.append(
            remote(
                own_kv.at[rows], window_ref.at[pl.ds(there, SEG)], halo_ss.at[s], halo_rs.at[s],
                left if s < 2 else right,
            )
        )
        halos[-1].start()
        locals_.append(
            pltpu.make_async_copy(own_kv.at[rows], window_ref.at[pl.ds(1024 + s * SEG, SEG)], local_sem.at[s])
        )
        locals_[-1].start()
    for s in range(4):
        for slot in range(4 * s, 4 * s + 4):

            @pl.when(slot != me)
            def _():
                remote(qg_in.at[slot], qg_in.at[slot], qg_ss.at[0], qg_rs.at[slot], left).wait_recv()

        rows = pl.ds(s * SEG, SEG)
        own_qg[rows, :] = jnp.dot(
            picks[s], qg_in[4 * s : 4 * s + 4].reshape(SEG, 128), preferred_element_type=jnp.float32
        ).astype(jnp.bfloat16)
        locals_.append(pltpu.make_async_copy(own_qg.at[rows], qg_ref.at[rows], local_sem.at[4 + s]))
        locals_[-1].start()
    for copy in halos:
        copy.wait()
    for copy in small + sends:
        copy.wait_send()
    for copy in locals_:
        copy.wait()


def attend_kernel(meta_ref, window_ref, qg_ref, aq_ref, own_ref, halo_ref, both, total):
    total[...] = jnp.zeros_like(total)
    low = lax.broadcasted_iota(jnp.int32, (BLK, 128), 1) < DIM

    def one_block(b, carry):
        seg, row = b // 4, b % 4
        live = meta_ref[seg, 4, row]
        steps = (live + 1) // 2
        rows = pl.ds(pl.multiple_of(b * BLK, BLK), BLK)
        qg = qg_ref[rows, :]
        zero = jnp.zeros_like(qg)
        pair = jnp.concatenate([jnp.where(low, qg, zero), jnp.where(low, zero, qg)], axis=0)

        def span(e):
            return pl.ds(pl.multiple_of((4 * seg + meta_ref[seg, row, e]) * BLK, BLK), BLK)

        def slot(e):
            return pl.ds(pl.multiple_of(e * BLK, BLK), BLK)

        def fold(x, op):
            return op(x.reshape(BLK // 8, 8, 128), axis=0)

        def scores(step, top):
            for u in range(2):
                e = 2 * step + u
                kv = window_ref[span(e), :]
                out = lax.dot_general(kv, pair, NT, preferred_element_type=jnp.float32)
                score = jnp.where(e < live, out[:, :BLK], -jnp.inf)
                both[slot(e), :BLK] = score
                both[slot(e), BLK:] = out[:, BLK:]
                top = jnp.maximum(top, fold(score, jnp.max))
            return top

        top = lax.fori_loop(0, steps, scores, jnp.full((8, 128), -jnp.inf, jnp.float32))
        top = jnp.max(top, axis=0, keepdims=True) * LOG2E

        def weigh(step, sums):
            mass, dot = sums
            for u in range(2):
                e = 2 * step + u
                part = jnp.exp2(both[slot(e), :BLK] * LOG2E - top)
                both[slot(e), :BLK] = part
                mass = mass + fold(part, jnp.sum)
                dot = dot + fold(part * both[slot(e), BLK:], jnp.sum)
            return mass, dot

        nought = jnp.zeros((8, 128), jnp.float32)
        mass, dot = lax.fori_loop(0, steps, weigh, (nought, nought))
        share = 1.0 / jnp.sum(mass, axis=0, keepdims=True)
        inner = jnp.sum(dot, axis=0, keepdims=True) * share

        def grads(step, acc):
            news = []
            for u in range(2):
                e = 2 * step + u
                chance = both[slot(e), :BLK] * share
                grad = chance * (both[slot(e), BLK:] - inner)
                w = jnp.concatenate([grad, chance], axis=1).astype(jnp.bfloat16)
                kv = window_ref[span(e), :]
                acc = acc + lax.dot_general(kv, w, TN, preferred_element_type=jnp.float32)
                news.append(total[span(e), :] + jnp.dot(w, pair, preferred_element_type=jnp.float32))
            for u in range(2):
                total[span(2 * step + u), :] = news[u]
            return acc

        acc = lax.fori_loop(0, steps, grads, jnp.zeros((128, 2 * BLK), jnp.float32))
        out = jnp.concatenate([acc[:DIM, :BLK] * SCALE, acc[DIM:, BLK:]], axis=0)
        aq_ref[rows, :] = jnp.transpose(out).astype(jnp.bfloat16)
        return carry

    lax.fori_loop(0, 16, one_block, 0)
    own_ref[...] = total[1024:3072, :]
    halo_ref[0:1024, :] = total[0:1024, :].astype(jnp.bfloat16)
    halo_ref[1024:2048, :] = total[3072:4096, :].astype(jnp.bfloat16)


def leave_kernel(
    aq_ref, own_ref, halo_ref, orders_ref,
    out_ref, dq_ref, dk_ref, dv_ref,
    aq_nat, kv_nat, halo_in, aq_in, kv_in,
    halo_ss, halo_rs, aq_ss, aq_rs, kv_ss, kv_rs,
):
    quad, me, left, right = place()
    greet(quad, me, left, right)
    half = pl.ds(0, 1024), pl.ds(1024, 1024)
    halos = [
        remote(halo_ref.at[half[0]], halo_in.at[half[1]], halo_ss.at[0], halo_rs.at[0], left),
        remote(halo_ref.at[half[1]], halo_in.at[half[0]], halo_ss.at[1], halo_rs.at[1], right),
    ]
    for copy in halos:
        copy.start()

    def one_hot(s):
        order = jnp.broadcast_to(orders_ref[s], (SEG, SEG))
        return (order == lax.broadcasted_iota(jnp.int32, (SEG, SEG), 0)).astype(jnp.bfloat16)

    def spread(nat, arrived, ssem, rsem, s):
        for part in range(4):
            slot = 4 * s + part
            copy = remote(
                nat.at[pl.ds(slot * BLK, BLK)], arrived.at[me], ssem.at[slot], rsem.at[me],
                member(quad, slot),
            )

            @pl.when(slot != me)
            def _():
                copy.start()

            @pl.when(slot == me)
            def _():
                arrived[me] = nat[pl.ds(slot * BLK, BLK), :]

    for s in range(4):
        rows = pl.ds(s * SEG, SEG)
        aq_nat[rows, :] = jnp.dot(
            one_hot(s), aq_ref[rows, :], preferred_element_type=jnp.float32
        ).astype(jnp.bfloat16)
        spread(aq_nat, aq_in, aq_ss, aq_rs, s)
    for h in (1, 0):
        halos[h].wait_recv()
        for s in (0, 1) if h == 1 else (2, 3):
            rows = pl.ds(s * SEG, SEG)
            whole = (own_ref[rows, :] + halo_in[rows, :].astype(jnp.float32)).astype(jnp.bfloat16)
            kv_nat[rows, :] = jnp.dot(
                one_hot(s), whole, preferred_element_type=jnp.float32
            ).astype(jnp.bfloat16)
            spread(kv_nat, kv_in, kv_ss, kv_rs, s)

    def collect(arrived, ssem, rsem, low_ref, high_ref):
        for slot in range(GROUP):

            @pl.when(slot != me)
            def _():
                remote(arrived.at[slot], arrived.at[slot], ssem.at[0], rsem.at[slot], left).wait_recv()

        for t in range(8):
            cols = slice(t * 128, t * 128 + 128)
            a, b = arrived[2 * t], arrived[2 * t + 1]
            low_ref[:, cols] = jnp.concatenate([a[:, :DIM], b[:, :DIM]], axis=1)
            high_ref[:, cols] = jnp.concatenate([a[:, DIM:], b[:, DIM:]], axis=1)

    collect(aq_in, aq_ss, aq_rs, dq_ref, out_ref)
    collect(kv_in, kv_ss, kv_rs, dk_ref, dv_ref)
    for copy in halos:
        copy.wait_send()
    for slot in range(GROUP):

        @pl.when(slot != me)
        def _():
            remote(aq_in.at[slot], aq_in.at[slot], aq_ss.at[slot], aq_rs.at[slot], left).wait_send()
            remote(kv_in.at[slot], kv_in.at[slot], kv_ss.at[slot], kv_rs.at[slot], left).wait_send()


def sems(*counts):
    return [pltpu.SemaphoreType.DMA((n,)) for n in counts]


def body(queries, keys, values, out_grad, node_order, block_lists, block_counts):
    bf, f32, i32 = jnp.bfloat16, jnp.float32, jnp.int32
    shape = jax.ShapeDtypeStruct
    slabs = pltpu.VMEM((GROUP, BLK, 128), bf)
    rows = pltpu.VMEM((4 * SEG, 128), bf)
    window, qg, orders, meta = pl.pallas_call(
        enter_kernel,
        out_shape=[
            shape((8 * SEG, 128), bf),
            shape((4 * SEG, 128), bf),
            shape((4, 1, SEG), i32),
            shape((4, 8, 128), i32),
        ],
        in_specs=[VMEM] * 7,
        out_specs=[ANY] * 4,
        scratch_shapes=[
            slabs, slabs, slabs, slabs, rows, rows,
            pltpu.VMEM((4, 1, SEG), i32), pltpu.VMEM((4, 8, 128), i32),
            *sems(16, 16, 16, 16, 4, 4, 4, 4, 4, 4, 10),
        ],
        compiler_params=pltpu.CompilerParams(
            collective_id=0, has_side_effects=True, vmem_limit_bytes=40 * 2**20
        ),
        name="enter",
    )(
        queries, keys, values, out_grad,
        node_order.reshape(1, SEG), block_lists, block_counts.reshape(1, 4),
    )
    aq, own, halo = pl.pallas_call(
        attend_kernel,
        out_shape=[shape((4 * SEG, 128), bf), shape((4 * SEG, 128), f32), shape((4 * SEG, 128), bf)],
        in_specs=[SMEM, VMEM, VMEM],
        out_specs=[VMEM] * 3,
        scratch_shapes=[pltpu.VMEM((LIST * BLK, 2 * BLK), f32), pltpu.VMEM((8 * SEG, 128), f32)],
        compiler_params=pltpu.CompilerParams(vmem_limit_bytes=40 * 2**20),
        name="attend",
    )(meta, window, qg)
    return pl.pallas_call(
        leave_kernel,
        out_shape=[shape((BLK, 16 * DIM), bf)] * 4,
        in_specs=[VMEM, VMEM, ANY, VMEM],
        out_specs=[VMEM] * 4,
        scratch_shapes=[
            rows, rows, rows, slabs, slabs,
            *sems(2, 2, 16, 16, 16, 16),
        ],
        compiler_params=pltpu.CompilerParams(
            collective_id=1, has_side_effects=True, vmem_limit_bytes=40 * 2**20
        ),
        name="leave",
    )(aq, own, halo, orders)


def solution(mesh):
    rows = P(("blk", "head"), None)
    return jax.shard_map(
        body,
        mesh=mesh,
        in_specs=(rows, rows, rows, rows, P("blk"), P("blk", None), P("blk")),
        out_specs=(rows, rows, rows, rows),
        check_vma=False,
    )
```

```python
import functools
import math

import jax
import jax.numpy as jnp
from jax import lax
from jax.experimental import pallas as pl
from jax.experimental.pallas import tpu as pltpu
from jax.sharding import PartitionSpec as P

BLK = 128
SEG = 512
DIM = 64
LIST = 12
UNROLL = 8
GROUP = 16
NT = (((1,), (1,)), ((), ()))
TN = (((0,), (0,)), ((), ()))
SCALE = 1.0 / math.sqrt(DIM)
LOG2E = math.log2(math.e)
MESH = pl.DeviceIdType.MESH
HBM = pl.BlockSpec(memory_space=pltpu.HBM)
VMEM = pl.BlockSpec(memory_space=pltpu.VMEM)
SMEM = pl.BlockSpec(memory_space=pltpu.SMEM)


def flip(slot, half):
    return slot + half * (2 - 4 * (slot // 2 % 2))


def place():
    blk, head = lax.axis_index("blk"), lax.axis_index("head")
    quads = lax.axis_size("blk") // 4
    quad, part = blk // 4, (blk % 4) * 4 + head
    half = quad // (quads // 2)
    role = flip(part, half)
    sides = []
    for step in (quads - 1, 1):
        there = lax.rem(quad + step, quads)
        sides.append(member(there, flip(role, there // (quads // 2))))
    return quad, half, part, role, sides[0], sides[1]


def member(quad, part):
    return (quad * 4 + part // 4, part % 4)


OTHERS = [(x, 1, c) for x in (0, 1, 2, 3) for c in (0, 1)]
OTHERS += [(x, 0, c) for x in (2, 1, 3) for c in (0, 1)] + [(0, 0, 1)]


def other(part, steps):
    x, y, c = part // 4, part // 2 % 2, part % 2
    dx, dy, dc = steps
    x = lax.rem(x + dx, 4)
    y = 1 - y if dy else y
    c = 1 - c if dc else c
    return x * 4 + y * 2 + c


def remote(src, dst, ssem, rsem, device):
    return pltpu.make_async_remote_copy(
        src_ref=src, dst_ref=dst, send_sem=ssem, recv_sem=rsem, device_id=device, device_id_type=MESH
    )


def greet(quad, part, left, right):
    barrier = pltpu.get_barrier_semaphore()
    for steps in OTHERS:
        pl.semaphore_signal(
            barrier, inc=1, device_id=member(quad, other(part, steps)), device_id_type=MESH
        )
    for device in (left, right):
        pl.semaphore_signal(barrier, inc=1, device_id=device, device_id_type=MESH)


def await_greetings():
    pl.semaphore_wait(pltpu.get_barrier_semaphore(), GROUP + 1)


def enter_kernel(
    q_hbm, k_hbm, v_hbm, g_hbm, order_hbm, lists_hbm, counts_hbm,
    window_ref, qg_ref, orders_ref, meta_ref,
    q_ref, k_ref, v_ref, g_ref, lists_ref, counts_ref,
    kv_out, qg_out, kv_in, qg_in, own_kv, order_in, meta_in,
    kv_ss, kv_rs, qg_ss, qg_rs, order_ss, order_rs, meta_ss, meta_rs, halo_ss, halo_rs, local_sem,
):
    quad, half, part, role, left, right = place()
    seg = part // 4
    pulls = [
        pltpu.make_async_copy(src, dst, local_sem.at[i])
        for i, (src, dst) in enumerate(
            (
                (k_hbm, k_ref), (v_hbm, v_ref), (lists_hbm, lists_ref), (counts_hbm, counts_ref),
                (order_hbm, order_in.at[seg]), (q_hbm, q_ref), (g_hbm, g_ref),
            )
        )
    ]
    for copy in pulls:
        copy.start()
    greet(quad, part, left, right)
    for copy in pulls[:2]:
        copy.wait()
    for t in range(8):
        cols = slice(t * 128, t * 128 + 128)
        k, v = k_ref[:, cols], v_ref[:, cols]
        kv_out[2 * t] = jnp.concatenate([k[:, :DIM], v[:, :DIM]], axis=1)
        kv_out[2 * t + 1] = jnp.concatenate([k[:, DIM:], v[:, DIM:]], axis=1)
    await_greetings()
    sends = []
    for i, steps in enumerate(OTHERS):
        there = other(part, steps)
        sends.append(
            remote(
                kv_out.at[flip(there, half)], kv_in.at[part], kv_ss.at[i], kv_rs.at[part],
                member(quad, there),
            )
        )
        sends[-1].start()
    for copy in pulls[2:5]:
        copy.wait()
    meta_in[seg] = jnp.zeros((8, 128), jnp.int32)
    meta_in[seg, 0:4, 0:LIST] = lists_ref[...]
    meta_in[seg, 4:5, 0:4] = counts_ref[...]
    for step in range(1, 4):
        peer = member(quad, other(part, (step, 0, 0)))
        for ref, ssem, rsem in ((order_in, order_ss, order_rs), (meta_in, meta_ss, meta_rs)):
            sends.append(remote(ref.at[seg], ref.at[seg], ssem.at[step], rsem.at[seg], peer))
            sends[-1].start()
    kv_in[part] = kv_out[role]
    for copy in pulls[5:]:
        copy.wait()
    for t in range(8):
        cols = slice(t * 128, t * 128 + 128)
        q, g = q_ref[:, cols] * SCALE, g_ref[:, cols]
        qg_out[2 * t] = jnp.concatenate([q[:, :DIM], g[:, :DIM]], axis=1)
        qg_out[2 * t + 1] = jnp.concatenate([q[:, DIM:], g[:, DIM:]], axis=1)
    for i, steps in enumerate(OTHERS):
        there = other(part, steps)
        sends.append(
            remote(
                qg_out.at[flip(there, half)], qg_in.at[part], qg_ss.at[i], qg_rs.at[part],
                member(quad, there),
            )
        )
        sends[-1].start()
    qg_in[part] = qg_out[role]

    for s in range(4):

        @pl.when(s != seg)
        def _():
            remote(order_in.at[s], order_in.at[s], order_ss.at[0], order_rs.at[s], left).wait_recv()
            remote(meta_in.at[s], meta_in.at[s], meta_ss.at[0], meta_rs.at[s], left).wait_recv()

    def one_hot(s):
        order = jnp.broadcast_to(order_in[s].astype(jnp.float32), (128, SEG))
        order = jnp.transpose(order)
        lane = lax.broadcasted_iota(jnp.int32, (SEG, 128), 1).astype(jnp.float32)
        tiles = [(order == lane + 128.0 * t).astype(jnp.bfloat16) for t in range(4)]
        return jnp.concatenate(tiles, axis=1)

    picks = [one_hot(s) for s in range(4)]
    orders_ref[...] = order_in[...]
    meta_ref[...] = meta_in[...]
    halos, keeps = [], []
    for s in range(4):
        for slot in range(4 * s, 4 * s + 4):

            @pl.when(slot != part)
            def _():
                remote(kv_in.at[slot], kv_in.at[slot], kv_ss.at[0], kv_rs.at[slot], left).wait_recv()

        rows = pl.ds(s * SEG, SEG)
        own_kv[rows, :] = jnp.dot(
            picks[s], kv_in[4 * s : 4 * s + 4].reshape(SEG, 128), preferred_element_type=jnp.float32
        ).astype(jnp.bfloat16)
        there = 3072 + s * SEG if s < 2 else (s - 2) * SEG
        halos.append(
            remote(
                own_kv.at[rows], window_ref.at[pl.ds(there, SEG)], halo_ss.at[s], halo_rs.at[s],
                left if s < 2 else right,
            )
        )
        halos[-1].start()
        keeps.append(
            pltpu.make_async_copy(own_kv.at[rows], window_ref.at[pl.ds(1024 + s * SEG, SEG)], local_sem.at[s])
        )
        keeps[-1].start()
    for s in range(4):
        for slot in range(4 * s, 4 * s + 4):

            @pl.when(slot != part)
            def _():
                remote(qg_in.at[slot], qg_in.at[slot], qg_ss.at[0], qg_rs.at[slot], left).wait_recv()

        qg_ref[pl.ds(s * SEG, SEG), :] = jnp.dot(
            picks[s], qg_in[4 * s : 4 * s + 4].reshape(SEG, 128), preferred_element_type=jnp.float32
        ).astype(jnp.bfloat16)
    for copy in halos + keeps:
        copy.wait()
    for copy in sends:
        copy.wait_send()


def attend_kernel(
    meta_ref, window_ref, qg_ref, aq_ref, total_ref,
    block_of, span_of, pairs, turned, both, acc, top, mass, dot,
):
    low = lax.broadcasted_iota(jnp.int32, (BLK, 128), 1) < DIM
    live = 0
    for b in range(16):
        for e in range(LIST):
            block_of[live + e] = b
            span_of[live + e] = (b // 4 * 4 + meta_ref[b // 4, b % 4, e]) * BLK
        live = live + meta_ref[b // 4, 4, b % 4]
    for u in range(UNROLL):
        block_of[live + u] = 16
        span_of[live + u] = 0
    steps = (live + UNROLL - 1) // UNROLL
    for b in range(16):
        qg = qg_ref[b * BLK : b * BLK + BLK, :]
        zero = jnp.zeros_like(qg)
        pairs[b, :BLK] = jnp.where(low, qg, zero)
        pairs[b, BLK:] = jnp.where(low, zero, qg)
    pairs[16] = jnp.zeros((2 * BLK, 128), jnp.bfloat16)
    for w in range(32):
        rows = slice(w * BLK, w * BLK + BLK)
        turned[rows, :] = jnp.transpose(window_ref[rows, :])
    total_ref[...] = jnp.zeros_like(total_ref)
    acc[...] = jnp.zeros_like(acc)
    top[...] = jnp.full(top.shape, -jnp.inf, jnp.float32)
    mass[...] = jnp.zeros_like(mass)
    dot[...] = jnp.zeros_like(dot)

    def tile(step, u):
        t = step * UNROLL + u
        return t, block_of[t], pl.ds(pl.multiple_of(span_of[t], BLK), BLK)

    def lay(x):
        return x.reshape(BLK // 8, 8, 128)

    def scores(step, carry):
        for u in range(UNROLL):
            t, b, span = tile(step, u)
            out = lax.dot_general(window_ref[span, :], pairs[b], NT, preferred_element_type=jnp.float32)
            both[t] = out
            top[b] = jnp.maximum(top[b], jnp.max(lay(out[:, :BLK]), axis=0))
        return carry

    lax.fori_loop(0, steps, scores, 0)
    top[...] = jnp.broadcast_to(jnp.max(top[...], axis=1, keepdims=True) * LOG2E, top.shape)

    def weigh(step, carry):
        for u in range(UNROLL):
            t, b, _ = tile(step, u)
            part = jnp.exp2(lay(both[t, :, :BLK]) * LOG2E - top[b])
            both[t, :, :BLK] = part.reshape(BLK, BLK)
            mass[b] = mass[b] + jnp.sum(part, axis=0)
            dot[b] = dot[b] + jnp.sum(part * lay(both[t, :, BLK:]), axis=0)
        return carry

    lax.fori_loop(0, steps, weigh, 0)
    share = 1.0 / jnp.sum(mass[...], axis=1, keepdims=True)
    dot[...] = jnp.broadcast_to(jnp.sum(dot[...], axis=1, keepdims=True) * share, dot.shape)
    mass[...] = jnp.broadcast_to(share, mass.shape)

    def grads(step, carry):
        for u in range(UNROLL):
            t, b, span = tile(step, u)
            chance = lay(both[t, :, :BLK]) * mass[b]
            grad = chance * (lay(both[t, :, BLK:]) - dot[b])
            w = jnp.concatenate([grad.reshape(BLK, BLK), chance.reshape(BLK, BLK)], axis=1)
            w = w.astype(jnp.bfloat16)
            out = jnp.dot(turned[span, :], w, preferred_element_type=jnp.float32)
            acc[b, :DIM] = acc[b, :DIM] + out[:DIM, :BLK]
            acc[b, DIM:] = acc[b, DIM:] + out[DIM:, BLK:]
            total_ref[span, :] = total_ref[span, :] + jnp.dot(
                w, pairs[b], preferred_element_type=jnp.float32
            )
        return carry

    lax.fori_loop(0, steps, grads, 0)
    for b in range(16):
        out = jnp.concatenate([acc[b, :DIM] * SCALE, acc[b, DIM:]], axis=0).astype(jnp.bfloat16)
        aq_ref[b * BLK : b * BLK + BLK, :] = jnp.transpose(out)


def leave_kernel(
    aq_ref, total_ref, orders_ref,
    aq_in, kv_in,
    aq_nat, kv_nat, halo_out, halo_in,
    halo_ss, halo_rs, aq_ss, aq_rs, kv_ss, kv_rs,
):
    quad, half, part, role, left, right = place()
    greet(quad, part, left, right)
    halo_out[0:1024, :] = total_ref[0:1024, :].astype(jnp.bfloat16)
    halo_out[1024:2048, :] = total_ref[3072:4096, :].astype(jnp.bfloat16)

    def one_hot(s):
        order = jnp.broadcast_to(orders_ref[s], (SEG, SEG))
        return (order == lax.broadcasted_iota(jnp.int32, (SEG, SEG), 0)).astype(jnp.bfloat16)

    def put(nat, rows, x, pick):
        nat[rows, :] = jnp.dot(pick, x, preferred_element_type=jnp.float32).astype(jnp.bfloat16)

    picks = [one_hot(s) for s in range(4)]
    await_greetings()
    halos = []
    for i in (0, 2, 1, 3):
        here, there = pl.ds(i * SEG, SEG), pl.ds((i + 2) % 4 * SEG, SEG)
        halos.append(
            remote(
                halo_out.at[here], halo_in.at[there], halo_ss.at[i], halo_rs.at[(i + 2) % 4],
                left if i < 2 else right,
            )
        )
        halos[-1].start()

    def spread(nat, arrived, ssem, rsem, s):
        for slot in range(4 * s, 4 * s + 4):

            @pl.when(slot != part)
            def _():
                remote(
                    nat.at[pl.ds(slot * BLK, BLK)], arrived.at[role], ssem.at[slot], rsem.at[role],
                    member(quad, slot),
                ).start()

            @pl.when(slot == part)
            def _():
                arrived[role] = nat[pl.ds(slot * BLK, BLK), :]

    for s in range(4):
        rows = pl.ds(s * SEG, SEG)
        put(aq_nat, rows, aq_ref[rows, :], picks[s])
        spread(aq_nat, aq_in, aq_ss, aq_rs, s)
    for s in (2, 0, 3, 1):
        rows = pl.ds(s * SEG, SEG)
        remote(halo_in.at[rows], halo_in.at[rows], halo_ss.at[s], halo_rs.at[s], left).wait_recv()
        whole = total_ref[pl.ds(1024 + s * SEG, SEG), :] + halo_in[rows, :].astype(jnp.float32)
        put(kv_nat, rows, whole.astype(jnp.bfloat16), picks[s])
        spread(kv_nat, kv_in, kv_ss, kv_rs, s)
    for copy in halos:
        copy.wait_send()
    for slot in range(GROUP):

        @pl.when(slot != part)
        def _():
            for arrived, ssem, rsem in ((aq_in, aq_ss, aq_rs), (kv_in, kv_ss, kv_rs)):
                there = arrived.at[slot]
                remote(there, there, ssem.at[slot], rsem.at[slot], left).wait_send()

        @pl.when(slot != role)
        def _():
            for arrived, ssem, rsem in ((aq_in, aq_ss, aq_rs), (kv_in, kv_ss, kv_rs)):
                there = arrived.at[slot]
                remote(there, there, ssem.at[slot], rsem.at[slot], left).wait_recv()


def finish_kernel(aq_ref, kv_ref, out_ref, dq_ref, dk_ref, dv_ref):
    for arrived, low_ref, high_ref in ((aq_ref, dq_ref, out_ref), (kv_ref, dk_ref, dv_ref)):
        for t in range(8):
            cols = slice(t * 128, t * 128 + 128)
            a, b = arrived[2 * t], arrived[2 * t + 1]
            low_ref[:, cols] = jnp.concatenate([a[:, :DIM], b[:, :DIM]], axis=1)
            high_ref[:, cols] = jnp.concatenate([a[:, DIM:], b[:, DIM:]], axis=1)


def sems(*counts):
    return [pltpu.SemaphoreType.DMA((n,)) for n in counts]


def body(queries, keys, values, out_grad, node_order, block_lists, block_counts):
    bf, f32, i32 = jnp.bfloat16, jnp.float32, jnp.int32
    shape = jax.ShapeDtypeStruct
    slabs = pltpu.VMEM((GROUP, BLK, 128), bf)
    rows = pltpu.VMEM((4 * SEG, 128), bf)
    mine = pltpu.VMEM((BLK, 16 * DIM), bf)
    window, qg, orders, meta = pl.pallas_call(
        enter_kernel,
        out_shape=[
            shape((8 * SEG, 128), bf),
            shape((4 * SEG, 128), bf),
            shape((4, 1, SEG), i32),
            shape((4, 8, 128), i32),
        ],
        in_specs=[HBM] * 7,
        out_specs=[VMEM] * 4,
        scratch_shapes=[
            mine, mine, mine, mine, pltpu.VMEM((4, LIST), i32), pltpu.VMEM((1, 4), i32),
            slabs, slabs, slabs, slabs, rows,
            pltpu.VMEM((4, 1, SEG), i32), pltpu.VMEM((4, 8, 128), i32),
            *sems(16, 16, 16, 16, 4, 4, 4, 4, 4, 4, 7),
        ],
        compiler_params=pltpu.CompilerParams(
            collective_id=0, has_side_effects=True, vmem_limit_bytes=16 * 2**20
        ),
        name="enter",
    )(
        *(
            pltpu.with_memory_space_constraint(x, pltpu.HBM)
            for x in (
                queries, keys, values, out_grad,
                node_order.reshape(1, SEG), block_lists, block_counts.reshape(1, 4),
            )
        )
    )
    stats = pltpu.VMEM((17, 8, 128), f32)
    aq, total = pl.pallas_call(
        attend_kernel,
        out_shape=[shape((4 * SEG, 128), bf), shape((8 * SEG, 128), f32)],
        in_specs=[SMEM, VMEM, VMEM],
        out_specs=[VMEM] * 2,
        scratch_shapes=[
            pltpu.SMEM((16 * LIST + 16,), i32), pltpu.SMEM((16 * LIST + 16,), i32),
            pltpu.VMEM((17, 2 * BLK, 128), bf), pltpu.VMEM((8 * SEG, 128), bf),
            pltpu.VMEM((16 * LIST + 8, BLK, 2 * BLK), f32), pltpu.VMEM((17, 128, BLK), f32),
            stats, stats, stats,
        ],
        compiler_params=pltpu.CompilerParams(vmem_limit_bytes=40 * 2**20),
        name="attend",
    )(meta, window, qg)
    aq_in, kv_in = pl.pallas_call(
        leave_kernel,
        out_shape=[shape((GROUP, BLK, 128), bf)] * 2,
        in_specs=[VMEM] * 3,
        out_specs=[VMEM] * 2,
        scratch_shapes=[rows, rows, rows, rows, *sems(4, 4, 16, 16, 16, 16)],
        compiler_params=pltpu.CompilerParams(
            collective_id=1, has_side_effects=True, vmem_limit_bytes=16 * 2**20
        ),
        name="leave",
    )(aq, total, orders)
    return pl.pallas_call(
        finish_kernel,
        out_shape=[shape((BLK, 16 * DIM), bf)] * 4,
        in_specs=[VMEM] * 2,
        out_specs=[VMEM] * 4,
        compiler_params=pltpu.CompilerParams(vmem_limit_bytes=8 * 2**20),
        name="finish",
    )(aq_in, kv_in)


def solution(mesh):
    rows = P(("blk", "head"), None)
    return jax.shard_map(
        body,
        mesh=mesh,
        in_specs=(rows, rows, rows, rows, P("blk"), P("blk", None), P("blk")),
        out_specs=(rows, rows, rows, rows),
        check_vma=False,
    )
```

```python
import functools
import math

import jax
import jax.numpy as jnp
from jax import lax
from jax.experimental import pallas as pl
from jax.experimental.pallas import tpu as pltpu
from jax.sharding import PartitionSpec as P

BLK = 128
SEG = 512
DIM = 64
LIST = 12
UNROLL = 16
GROUP = 16
NT = (((1,), (1,)), ((), ()))
TN = (((0,), (0,)), ((), ()))
SCALE = 1.0 / math.sqrt(DIM)
LOG2E = math.log2(math.e)
MESH = pl.DeviceIdType.MESH
HBM = pl.BlockSpec(memory_space=pltpu.HBM)
VMEM = pl.BlockSpec(memory_space=pltpu.VMEM)
SMEM = pl.BlockSpec(memory_space=pltpu.SMEM)


def flip(slot, half):
    return slot + half * (2 - 4 * (slot // 2 % 2))


def place():
    blk, head = lax.axis_index("blk"), lax.axis_index("head")
    quads = lax.axis_size("blk") // 4
    quad, part = blk // 4, (blk % 4) * 4 + head
    half = quad // (quads // 2)
    role = flip(part, half)
    sides = []
    for step in (quads - 1, 1):
        there = lax.rem(quad + step, quads)
        sides.append(member(there, flip(role, there // (quads // 2))))
    return quad, half, part, role, sides[0], sides[1]


def member(quad, part):
    return (quad * 4 + part // 4, part % 4)


OTHERS = [
    (2, 1, 0), (2, 0, 0), (1, 1, 0), (3, 1, 0), (2, 1, 1), (2, 0, 1), (1, 0, 0), (3, 0, 0),
    (0, 1, 0), (1, 1, 1), (3, 1, 1), (0, 1, 1), (1, 0, 1), (3, 0, 1), (0, 0, 1),
]


def other(part, steps):
    x, y, c = part // 4, part // 2 % 2, part % 2
    dx, dy, dc = steps
    x = lax.rem(x + dx, 4)
    y = 1 - y if dy else y
    c = 1 - c if dc else c
    return x * 4 + y * 2 + c


def remote(src, dst, ssem, rsem, device):
    return pltpu.make_async_remote_copy(
        src_ref=src, dst_ref=dst, send_sem=ssem, recv_sem=rsem, device_id=device, device_id_type=MESH
    )


def greet(quad, part, left, right):
    barrier = pltpu.get_barrier_semaphore()
    for steps in OTHERS:
        pl.semaphore_signal(
            barrier, inc=1, device_id=member(quad, other(part, steps)), device_id_type=MESH
        )
    for device in (left, right):
        pl.semaphore_signal(barrier, inc=1, device_id=device, device_id_type=MESH)


def await_greetings():
    pl.semaphore_wait(pltpu.get_barrier_semaphore(), GROUP + 1)


def enter_kernel(
    q_hbm, k_hbm, v_hbm, g_hbm, order_hbm, lists_hbm, counts_hbm,
    window_ref, turned_ref, pairs_ref, meta_ref,
    q_ref, k_ref, v_ref, g_ref, order_ref, lists_ref, counts_ref,
    kv_out, qg_out, kv_in, qg_in, halo_in, meta_in, meta_halo, picks,
    kv_ss, kv_rs, qg_ss, qg_rs, halo_ss, halo_rs, meta_ss, meta_rs, side_ss, side_rs, local_sem,
):
    quad, half, part, role, left, right = place()
    seg = part // 4
    pulls = [
        pltpu.make_async_copy(src, dst, local_sem.at[i])
        for i, (src, dst) in enumerate(
            (
                (order_hbm, order_ref), (lists_hbm, lists_ref), (counts_hbm, counts_ref),
                (k_hbm, k_ref), (v_hbm, v_ref), (q_hbm, q_ref), (g_hbm, g_ref),
            )
        )
    ]
    for copy in pulls:
        copy.start()
    greet(quad, part, left, right)
    for copy in pulls[:3]:
        copy.wait()
    meta_in[seg] = jnp.zeros((16, 128), jnp.int32)
    for t in range(4):
        meta_in[seg, t : t + 1, :] = order_ref[:, t * 128 : t * 128 + 128]
    meta_in[seg, 4:8, 0:LIST] = lists_ref[...]
    meta_in[seg, 8:9, 0:4] = counts_ref[...]
    for copy in pulls[3:5]:
        copy.wait()
    for t in range(8):
        cols = slice(t * 128, t * 128 + 128)
        k, v = k_ref[:, cols], v_ref[:, cols]
        kv_out[2 * t] = jnp.concatenate([k[:, :DIM], v[:, :DIM]], axis=1)
        kv_out[2 * t + 1] = jnp.concatenate([k[:, DIM:], v[:, DIM:]], axis=1)
    await_greetings()
    sends = []

    def send(src, dst, ssem, rsem, device):
        sends.append(remote(src, dst, ssem, rsem, device))
        sends[-1].start()

    def scatter(i, out, arrived, ssem, rsem):
        there = other(part, OTHERS[i])
        send(out.at[flip(there, half)], arrived.at[part], ssem.at[i], rsem.at[part], member(quad, there))

    def landed(ref, rsem, slot):
        remote(ref.at[slot], ref.at[slot], kv_ss.at[0], rsem.at[slot], left).wait_recv()

    def pass_on(slot):
        device = [jnp.where(slot < 8, a, b) for a, b in zip(left, right)]
        there = lax.rem(slot + 8, GROUP)
        remote(kv_in.at[slot], halo_in.at[there], halo_ss.at[slot], halo_rs.at[there], device).start()

    for step in range(1, 4):
        peer = member(quad, other(part, (step, 0, 0)))
        send(meta_in.at[seg], meta_in.at[seg], meta_ss.at[step], meta_rs.at[seg], peer)
    for i in range(len(OTHERS)):
        scatter(i, kv_out, kv_in, kv_ss, kv_rs)
    kv_in[part] = kv_out[role]
    pass_on(part)
    for copy in pulls[5:]:
        copy.wait()
    for t in range(8):
        cols = slice(t * 128, t * 128 + 128)
        q, g = q_ref[:, cols] * SCALE, g_ref[:, cols]
        qg_out[2 * t] = jnp.concatenate([q[:, :DIM], g[:, :DIM]], axis=1)
        qg_out[2 * t + 1] = jnp.concatenate([q[:, DIM:], g[:, DIM:]], axis=1)
    for i in range(len(OTHERS)):
        scatter(i, qg_out, qg_in, qg_ss, qg_rs)
    qg_in[part] = qg_out[role]
    for step in range(1, 4):
        landed(meta_in, meta_rs, lax.rem(seg + step, 4))

    send(meta_in.at[0:2], meta_halo.at[2:4], side_ss.at[0], side_rs.at[1], left)
    send(meta_in.at[2:4], meta_halo.at[0:2], side_ss.at[1], side_rs.at[0], right)
    lane = lax.broadcasted_iota(jnp.int32, (SEG, 128), 1).astype(jnp.float32)

    def one_hot(at, meta):
        rows = meta[0:4].astype(jnp.float32)
        order = jnp.concatenate(
            [jnp.transpose(jnp.broadcast_to(rows[t : t + 1], (128, 128))) for t in range(4)], axis=0
        )
        for t in range(4):
            picks[at, :, t * 128 : t * 128 + 128] = (order == lane + 128.0 * t).astype(jnp.bfloat16)

    meta_ref[...] = meta_in[...]
    for dx, dy, dc in OTHERS:
        slot = other(part, (-dx % 4, dy, dc))
        landed(kv_in, kv_rs, slot)
        pass_on(slot)

    def blocked(pick, arrived, s):
        rows = arrived[4 * s : 4 * s + 4].reshape(SEG, 128)
        return jnp.dot(picks[pick], rows, preferred_element_type=jnp.float32).astype(jnp.bfloat16)

    def keep(at, kv):
        window_ref[at : at + SEG, :] = kv
        for i in range(0, SEG, BLK):
            turned_ref[at + i : at + i + BLK, :] = jnp.transpose(kv[i : i + BLK])

    for s in range(4):
        one_hot(s, meta_in[s])
    for side in range(2):
        two = meta_halo.at[2 * side : 2 * side + 2]
        remote(two, two, side_ss.at[side], side_rs.at[side], left).wait_recv()
        for s in (2 * side, 2 * side + 1):
            one_hot(4 + s, meta_halo[s])
    for s in range(4):
        keep(1024 + s * SEG, blocked(s, kv_in, s))
    for dx, dy, dc in OTHERS:
        landed(qg_in, qg_rs, other(part, (-dx % 4, dy, dc)))
    for slot in range(GROUP):
        landed(halo_in, halo_rs, slot)
    low = lax.broadcasted_iota(jnp.int32, (SEG, 128), 1) < DIM
    for s in range(4):
        qg = blocked(s, qg_in, s)
        zero = jnp.zeros_like(qg)
        pairs_ref[4 * s : 4 * s + 4, :BLK] = jnp.where(low, qg, zero).reshape(4, BLK, 128)
        pairs_ref[4 * s : 4 * s + 4, BLK:] = jnp.where(low, zero, qg).reshape(4, BLK, 128)
        keep((s if s < 2 else s + 4) * SEG, blocked(4 + s, halo_in, s))
    pairs_ref[16] = jnp.zeros((2 * BLK, 128), jnp.bfloat16)
    for copy in sends:
        copy.wait_send()
    for slot in range(GROUP):
        remote(kv_in.at[slot], kv_in.at[slot], halo_ss.at[slot], halo_rs.at[slot], left).wait_send()


def attend_kernel(
    meta_ref, window_ref, turned_ref, pairs, aq_ref, total_ref,
    block_of, first_of, second_of, whole_of, both, acc, top, mass, dot,
):
    live = 0
    for b in range(16):
        count = meta_ref[b // 4, 8, b % 4]
        for i in range(LIST // 2):
            block_of[live + i] = b
            first_of[live + i] = (b // 4 * 4 + meta_ref[b // 4, 4 + b % 4, 2 * i]) * BLK
            second_of[live + i] = (b // 4 * 4 + meta_ref[b // 4, 4 + b % 4, 2 * i + 1]) * BLK
            whole_of[live + i] = count - 2 * i - 1
        live = live + (count + 1) // 2
    for u in range(UNROLL):
        block_of[live + u] = 16
        first_of[live + u] = 0
        second_of[live + u] = BLK
        whole_of[live + u] = 0
    steps = (live + UNROLL - 1) // UNROLL
    total_ref[...] = jnp.zeros_like(total_ref)
    acc[...] = jnp.zeros_like(acc)
    top[...] = jnp.full(top.shape, -jnp.inf, jnp.float32)
    mass[...] = jnp.zeros_like(mass)
    dot[...] = jnp.zeros_like(dot)

    def tiles(step, u):
        t = step * UNROLL + u
        spans = [pl.ds(pl.multiple_of(ref[t], BLK), BLK) for ref in (first_of, second_of)]
        return t, block_of[t], spans[0], spans[1], whole_of[t] > 0

    def lay(x):
        return x.reshape(BLK // 8, 8, 128)

    def scores(step, carry):
        for u in range(UNROLL):
            t, b, one, two, whole = tiles(step, u)
            kv = jnp.concatenate([window_ref[one, :], window_ref[two, :]], axis=0)
            out = lax.dot_general(kv, pairs[b], NT, preferred_element_type=jnp.float32)
            both[t] = out
            high = jnp.max(lay(out[:BLK, :BLK]), axis=0)
            other_high = jnp.max(lay(out[BLK:, :BLK]), axis=0)
            high = jnp.maximum(high, jnp.where(whole, other_high, -jnp.inf))
            top[b] = jnp.maximum(top[b], high)
        return carry

    lax.fori_loop(0, steps, scores, 0)
    top[...] = jnp.broadcast_to(jnp.max(top[...], axis=1, keepdims=True) * LOG2E, top.shape)

    def weigh(step, carry):
        for u in range(UNROLL):
            t, b, _, _, whole = tiles(step, u)
            high = top[b]
            one = jnp.exp2(lay(both[t, :BLK, :BLK]) * LOG2E - high)
            two = jnp.exp2(lay(both[t, BLK:, :BLK]) * LOG2E - jnp.where(whole, high, jnp.inf))
            both[t, :BLK, :BLK] = one.reshape(BLK, BLK)
            both[t, BLK:, :BLK] = two.reshape(BLK, BLK)
            mass[b] = mass[b] + jnp.sum(one + two, axis=0)
            dot[b] = dot[b] + jnp.sum(
                one * lay(both[t, :BLK, BLK:]) + two * lay(both[t, BLK:, BLK:]), axis=0
            )
        return carry

    lax.fori_loop(0, steps, weigh, 0)
    share = 1.0 / jnp.sum(mass[...], axis=1, keepdims=True)
    dot[...] = jnp.broadcast_to(jnp.sum(dot[...], axis=1, keepdims=True) * share, dot.shape)
    mass[...] = jnp.broadcast_to(share, mass.shape)

    def grads(step, carry):
        for u in range(UNROLL):
            t, b, one, two, _ = tiles(step, u)
            chance = both[t, :, :BLK].reshape(BLK // 4, 8, 128) * mass[b]
            grad = chance * (both[t, :, BLK:].reshape(BLK // 4, 8, 128) - dot[b])
            w = jnp.concatenate([grad.reshape(2 * BLK, BLK), chance.reshape(2 * BLK, BLK)], axis=1)
            w = w.astype(jnp.bfloat16)
            kv = jnp.concatenate([turned_ref[one, :], turned_ref[two, :]], axis=1)
            out = jnp.dot(kv, w, preferred_element_type=jnp.float32)
            acc[b, :DIM] = acc[b, :DIM] + out[:DIM, :BLK]
            acc[b, DIM:] = acc[b, DIM:] + out[DIM:, BLK:]
            out = jnp.dot(w, pairs[b], preferred_element_type=jnp.float32)
            one_sum, two_sum = total_ref[one, :] + out[:BLK], total_ref[two, :] + out[BLK:]
            total_ref[one, :] = one_sum
            total_ref[two, :] = two_sum
        return carry

    lax.fori_loop(0, steps, grads, 0)
    for b in range(16):
        out = jnp.concatenate([acc[b, :DIM] * SCALE, acc[b, DIM:]], axis=0).astype(jnp.bfloat16)
        aq_ref[b * BLK : b * BLK + BLK, :] = jnp.transpose(out)


def leave_kernel(
    aq_ref, total_ref, meta_ref,
    aq_in, kv_in,
    aq_nat, kv_nat, halo_out, halo_in, picks,
    halo_ss, halo_rs, aq_ss, aq_rs, kv_ss, kv_rs,
):
    quad, half, part, role, left, right = place()
    greet(quad, part, left, right)
    halo_out[0:8] = total_ref[0:1024, :].astype(jnp.bfloat16).reshape(8, BLK, 128)
    halo_out[8:16] = total_ref[3072:4096, :].astype(jnp.bfloat16).reshape(8, BLK, 128)

    def natural(nat, s, x):
        x = jnp.dot(picks[s], x, preferred_element_type=jnp.float32).astype(jnp.bfloat16)
        nat[pl.ds(4 * s, 4)] = x.reshape(4, BLK, 128)

    for s in range(4):
        order = jnp.concatenate([meta_ref[s, t : t + 1, :] for t in range(4)], axis=1)
        here = lax.broadcasted_iota(jnp.int32, (SEG, SEG), 0)
        picks[s] = (jnp.broadcast_to(order, (SEG, SEG)) == here).astype(jnp.bfloat16)
        natural(aq_nat, s, aq_ref[s * SEG : s * SEG + SEG, :])
    await_greetings()
    turn = [lax.rem(part // 4 + d, 4) for d in (2, 1, 3, 0)]
    for i in range(GROUP):
        there = 4 * turn[i // 4] + i % 4
        here = lax.rem(there + 8, GROUP)
        device = [jnp.where(here < 8, a, b) for a, b in zip(left, right)]
        remote(halo_out.at[here], halo_in.at[there], halo_ss.at[here], halo_rs.at[there], device).start()
        if i < len(OTHERS):
            slot = other(part, OTHERS[i])
            remote(
                aq_nat.at[slot], aq_in.at[role], aq_ss.at[slot], aq_rs.at[role], member(quad, slot)
            ).start()
    aq_in[role] = aq_nat[part]
    for s, dx in zip(turn, (2, 1, 3, 0)):
        for p in range(4):
            piece = halo_in.at[4 * s + p]
            remote(piece, piece, halo_ss.at[0], halo_rs.at[4 * s + p], left).wait_recv()
        arrived = halo_in[pl.ds(4 * s, 4)].reshape(SEG, 128).astype(jnp.float32)
        whole = total_ref[pl.ds(pl.multiple_of(1024 + s * SEG, SEG), SEG), :] + arrived
        natural(kv_nat, s, whole.astype(jnp.bfloat16))
        for dy, dc in ((1, 0), (0, 1), (1, 1), (0, 0)):
            if (dx, dy, dc) != (0, 0, 0):
                slot = other(part, (dx, dy, dc))
                remote(
                    kv_nat.at[slot], kv_in.at[role], kv_ss.at[slot], kv_rs.at[role], member(quad, slot)
                ).start()
    kv_in[role] = kv_nat[part]
    for slot in range(GROUP):
        remote(halo_out.at[slot], halo_out.at[slot], halo_ss.at[slot], halo_rs.at[0], left).wait_send()

        @pl.when(slot != part)
        def _():
            for arrived, ssem, rsem in ((aq_in, aq_ss, aq_rs), (kv_in, kv_ss, kv_rs)):
                there = arrived.at[slot]
                remote(there, there, ssem.at[slot], rsem.at[slot], left).wait_send()

        @pl.when(slot != role)
        def _():
            for arrived, ssem, rsem in ((aq_in, aq_ss, aq_rs), (kv_in, kv_ss, kv_rs)):
                there = arrived.at[slot]
                remote(there, there, ssem.at[slot], rsem.at[slot], left).wait_recv()


def finish_kernel(aq_ref, kv_ref, out_ref, dq_ref, dk_ref, dv_ref):
    for arrived, low_ref, high_ref in ((aq_ref, dq_ref, out_ref), (kv_ref, dk_ref, dv_ref)):
        for t in range(8):
            cols = slice(t * 128, t * 128 + 128)
            a, b = arrived[2 * t], arrived[2 * t + 1]
            low_ref[:, cols] = jnp.concatenate([a[:, :DIM], b[:, :DIM]], axis=1)
            high_ref[:, cols] = jnp.concatenate([a[:, DIM:], b[:, DIM:]], axis=1)


def sems(*counts):
    return [pltpu.SemaphoreType.DMA((n,)) for n in counts]


def body(queries, keys, values, out_grad, node_order, block_lists, block_counts):
    bf, f32, i32 = jnp.bfloat16, jnp.float32, jnp.int32
    shape = jax.ShapeDtypeStruct
    slabs = pltpu.VMEM((GROUP, BLK, 128), bf)
    numbers = pltpu.VMEM((4, 16, 128), i32)
    mine = pltpu.VMEM((BLK, 16 * DIM), bf)
    window, turned, pairs, meta = pl.pallas_call(
        enter_kernel,
        out_shape=[
            shape((8 * SEG, 128), bf),
            shape((8 * SEG, 128), bf),
            shape((17, 2 * BLK, 128), bf),
            shape((4, 16, 128), i32),
        ],
        in_specs=[HBM] * 7,
        out_specs=[VMEM] * 4,
        scratch_shapes=[
            mine, mine, mine, mine,
            pltpu.VMEM((1, SEG), i32), pltpu.VMEM((4, LIST), i32), pltpu.VMEM((1, 4), i32),
            slabs, slabs, slabs, slabs, slabs, numbers, numbers, pltpu.VMEM((8, SEG, SEG), bf),
            *sems(16, 16, 16, 16, 16, 16, 4, 4, 2, 2, 7),
        ],
        compiler_params=pltpu.CompilerParams(
            collective_id=0, has_side_effects=True, vmem_limit_bytes=16 * 2**20
        ),
        name="enter",
    )(
        *(
            pltpu.with_memory_space_constraint(x, pltpu.HBM)
            for x in (
                queries, keys, values, out_grad,
                node_order.reshape(1, SEG), block_lists, block_counts.reshape(1, 4),
            )
        )
    )
    stats = pltpu.VMEM((17, 8, 128), f32)
    pairs_most = 8 * LIST + 16
    table = pltpu.SMEM((pairs_most,), i32)
    aq, total = pl.pallas_call(
        attend_kernel,
        out_shape=[shape((4 * SEG, 128), bf), shape((8 * SEG, 128), f32)],
        in_specs=[SMEM, VMEM, VMEM, VMEM],
        out_specs=[VMEM] * 2,
        scratch_shapes=[
            table, table, table, table,
            pltpu.VMEM((pairs_most, 2 * BLK, 2 * BLK), f32), pltpu.VMEM((17, 128, BLK), f32),
            stats, stats, stats,
        ],
        compiler_params=pltpu.CompilerParams(vmem_limit_bytes=40 * 2**20),
        name="attend",
    )(meta, window, turned, pairs)
    aq_in, kv_in = pl.pallas_call(
        leave_kernel,
        out_shape=[shape((GROUP, BLK, 128), bf)] * 2,
        in_specs=[VMEM] * 3,
        out_specs=[VMEM] * 2,
        scratch_shapes=[
            slabs, slabs, slabs, slabs, pltpu.VMEM((4, SEG, SEG), bf),
            *sems(16, 16, 16, 16, 16, 16),
        ],
        compiler_params=pltpu.CompilerParams(
            collective_id=1, has_side_effects=True, vmem_limit_bytes=16 * 2**20
        ),
        name="leave",
    )(aq, total, meta)
    return pl.pallas_call(
        finish_kernel,
        out_shape=[shape((BLK, 16 * DIM), bf)] * 4,
        in_specs=[VMEM] * 2,
        out_specs=[VMEM] * 4,
        compiler_params=pltpu.CompilerParams(vmem_limit_bytes=8 * 2**20),
        name="finish",
    )(aq_in, kv_in)


def solution(mesh):
    rows = P(("blk", "head"), None)
    return jax.shard_map(
        body,
        mesh=mesh,
        in_specs=(rows, rows, rows, rows, P("blk"), P("blk", None), P("blk")),
        out_specs=(rows, rows, rows, rows),
        check_vma=False,
    )
```

```python
import functools
import math

import jax
import jax.numpy as jnp
from jax import lax
from jax.experimental import pallas as pl
from jax.experimental.pallas import tpu as pltpu
from jax.sharding import PartitionSpec as P

BLK = 128
SEG = 512
DIM = 64
LIST = 12
UNROLL = 40
REST = 8
GROUP = 16
NT = (((1,), (1,)), ((), ()))
TN = (((0,), (0,)), ((), ()))
SCALE = 1.0 / math.sqrt(DIM)
LOG2E = math.log2(math.e)
MESH = pl.DeviceIdType.MESH
HBM = pl.BlockSpec(memory_space=pltpu.HBM)
VMEM = pl.BlockSpec(memory_space=pltpu.VMEM)
SMEM = pl.BlockSpec(memory_space=pltpu.SMEM)


def flip(slot, half):
    return slot + half * (2 - 4 * (slot // 2 % 2))


def place():
    blk, head = lax.axis_index("blk"), lax.axis_index("head")
    quads = lax.axis_size("blk") // 4
    quad, part = blk // 4, (blk % 4) * 4 + head
    half = quad // (quads // 2)
    role = flip(part, half)
    sides = []
    for step in (quads - 1, 1):
        there = lax.rem(quad + step, quads)
        sides.append(member(there, flip(role, there // (quads // 2))))
    return quad, half, part, role, sides[0], sides[1]


def member(quad, part):
    return (quad * 4 + part // 4, part % 4)


OTHERS = [
    (2, 1, 0), (2, 0, 0), (1, 1, 0), (3, 1, 0), (2, 1, 1), (2, 0, 1), (1, 0, 0), (3, 0, 0),
    (0, 1, 0), (1, 1, 1), (3, 1, 1), (0, 1, 1), (1, 0, 1), (3, 0, 1), (0, 0, 1),
]


def other(part, steps):
    x, y, c = part // 4, part // 2 % 2, part % 2
    dx, dy, dc = steps
    x = lax.rem(x + dx, 4)
    y = 1 - y if dy else y
    c = 1 - c if dc else c
    return x * 4 + y * 2 + c


def remote(src, dst, ssem, rsem, device):
    return pltpu.make_async_remote_copy(
        src_ref=src, dst_ref=dst, send_sem=ssem, recv_sem=rsem, device_id=device, device_id_type=MESH
    )


def greet(quad, part, left, right):
    barrier = pltpu.get_barrier_semaphore()
    for steps in OTHERS:
        pl.semaphore_signal(
            barrier, inc=1, device_id=member(quad, other(part, steps)), device_id_type=MESH
        )
    for device in (left, right):
        pl.semaphore_signal(barrier, inc=1, device_id=device, device_id_type=MESH)


def await_greetings():
    pl.semaphore_wait(pltpu.get_barrier_semaphore(), GROUP + 1)


def enter_kernel(
    q_hbm, k_hbm, v_hbm, g_hbm, order_hbm, lists_hbm, counts_hbm,
    window_ref, turned_ref, pairs_ref, meta_ref, table_ref,
    q_ref, k_ref, v_ref, g_ref, order_ref, lists_ref, counts_ref,
    kv_out, qg_out, kv_in, qg_in, halo_in, meta_in, meta_halo, picks,
    kv_ss, kv_rs, qg_ss, qg_rs, halo_ss, halo_rs, meta_ss, meta_rs, side_ss, side_rs, local_sem,
):
    quad, half, part, role, left, right = place()
    seg = part // 4
    pulls = [
        pltpu.make_async_copy(src, dst, local_sem.at[i])
        for i, (src, dst) in enumerate(
            (
                (order_hbm, order_ref), (lists_hbm, lists_ref), (counts_hbm, counts_ref),
                (k_hbm, k_ref), (v_hbm, v_ref), (q_hbm, q_ref), (g_hbm, g_ref),
            )
        )
    ]
    for copy in pulls:
        copy.start()
    greet(quad, part, left, right)
    for copy in pulls[:3]:
        copy.wait()
    meta_in[seg] = jnp.zeros((16, 128), jnp.int32)
    for t in range(4):
        meta_in[seg, t : t + 1, :] = order_ref[:, t * 128 : t * 128 + 128]
    meta_in[seg, 4:8, 0:LIST] = lists_ref[...]
    meta_in[seg, 8:9, 0:4] = counts_ref[...]
    for copy in pulls[3:5]:
        copy.wait()
    for t in range(8):
        cols = slice(t * 128, t * 128 + 128)
        k, v = k_ref[:, cols], v_ref[:, cols]
        kv_out[2 * t] = jnp.concatenate([k[:, :DIM], v[:, :DIM]], axis=1)
        kv_out[2 * t + 1] = jnp.concatenate([k[:, DIM:], v[:, DIM:]], axis=1)
    await_greetings()
    sends = []

    def send(src, dst, ssem, rsem, device):
        sends.append(remote(src, dst, ssem, rsem, device))
        sends[-1].start()

    def scatter(i, out, arrived, ssem, rsem):
        there = other(part, OTHERS[i])
        send(out.at[flip(there, half)], arrived.at[part], ssem.at[i], rsem.at[part], member(quad, there))

    def landed(ref, rsem, slot):
        remote(ref.at[slot], ref.at[slot], kv_ss.at[0], rsem.at[slot], left).wait_recv()

    def pass_on(slot):
        device = [jnp.where(slot < 8, a, b) for a, b in zip(left, right)]
        there = lax.rem(slot + 8, GROUP)
        remote(kv_in.at[slot], halo_in.at[there], halo_ss.at[slot], halo_rs.at[there], device).start()

    for step in range(1, 4):
        peer = member(quad, other(part, (step, 0, 0)))
        send(meta_in.at[seg], meta_in.at[seg], meta_ss.at[step], meta_rs.at[seg], peer)
    for i in range(len(OTHERS)):
        scatter(i, kv_out, kv_in, kv_ss, kv_rs)
    kv_in[part] = kv_out[role]
    pass_on(part)
    for copy in pulls[5:]:
        copy.wait()
    for t in range(8):
        cols = slice(t * 128, t * 128 + 128)
        q, g = q_ref[:, cols] * SCALE, g_ref[:, cols]
        qg_out[2 * t] = jnp.concatenate([q[:, :DIM], g[:, :DIM]], axis=1)
        qg_out[2 * t + 1] = jnp.concatenate([q[:, DIM:], g[:, DIM:]], axis=1)
    for i in range(len(OTHERS)):
        scatter(i, qg_out, qg_in, qg_ss, qg_rs)
    qg_in[part] = qg_out[role]
    for step in range(1, 4):
        landed(meta_in, meta_rs, lax.rem(seg + step, 4))

    send(meta_in.at[0:2], meta_halo.at[2:4], side_ss.at[0], side_rs.at[1], left)
    send(meta_in.at[2:4], meta_halo.at[0:2], side_ss.at[1], side_rs.at[0], right)
    lane = lax.broadcasted_iota(jnp.int32, (SEG, 128), 1).astype(jnp.float32)

    def one_hot(at, meta):
        rows = meta[0:4].astype(jnp.float32)
        order = jnp.concatenate(
            [jnp.transpose(jnp.broadcast_to(rows[t : t + 1], (128, 128))) for t in range(4)], axis=0
        )
        for t in range(4):
            picks[at, :, t * 128 : t * 128 + 128] = (order == lane + 128.0 * t).astype(jnp.bfloat16)

    meta_ref[...] = meta_in[...]
    table_ref[...] = jnp.zeros((24, 128), jnp.int32)
    for s in range(4):
        table_ref[4 * s : 4 * s + 4, :] = meta_in[s, 4:8, :]
        table_ref[16 + s : 17 + s, :] = meta_in[s, 8:9, :]
    for dx, dy, dc in OTHERS:
        slot = other(part, (-dx % 4, dy, dc))
        landed(kv_in, kv_rs, slot)
        pass_on(slot)

    def blocked(pick, arrived, s):
        rows = arrived[4 * s : 4 * s + 4].reshape(SEG, 128)
        return jnp.dot(picks[pick], rows, preferred_element_type=jnp.float32).astype(jnp.bfloat16)

    def keep(at, kv):
        window_ref[at : at + SEG, :] = kv
        for i in range(0, SEG, BLK):
            turned_ref[at + i : at + i + BLK, :] = jnp.transpose(kv[i : i + BLK])

    for s in range(4):
        one_hot(s, meta_in[s])
    for side in range(2):
        two = meta_halo.at[2 * side : 2 * side + 2]
        remote(two, two, side_ss.at[side], side_rs.at[side], left).wait_recv()
        for s in (2 * side, 2 * side + 1):
            one_hot(4 + s, meta_halo[s])
    for s in range(4):
        keep(1024 + s * SEG, blocked(s, kv_in, s))
    for dx, dy, dc in OTHERS:
        landed(qg_in, qg_rs, other(part, (-dx % 4, dy, dc)))
    low = lax.broadcasted_iota(jnp.int32, (SEG, 128), 1) < DIM
    for s in range(4):
        qg = blocked(s, qg_in, s)
        zero = jnp.zeros_like(qg)
        pairs_ref[4 * s : 4 * s + 4, :BLK] = jnp.where(low, qg, zero).reshape(4, BLK, 128)
        pairs_ref[4 * s : 4 * s + 4, BLK:] = jnp.where(low, zero, qg).reshape(4, BLK, 128)
    for slot in range(GROUP):
        landed(halo_in, halo_rs, slot)
    for s in range(4):
        keep((s if s < 2 else s + 4) * SEG, blocked(4 + s, halo_in, s))
    pairs_ref[16] = jnp.zeros((2 * BLK, 128), jnp.bfloat16)
    for copy in sends:
        copy.wait_send()
    for slot in range(GROUP):
        remote(kv_in.at[slot], kv_in.at[slot], halo_ss.at[slot], halo_rs.at[slot], left).wait_send()


def attend_kernel(
    lists_ref, window_ref, turned_ref, pairs, aq_ref, total_ref,
    code_of, part, change, high_of, acc, top, mass, dot,
):
    live = 0
    for b in range(16):
        count = lists_ref[16 + b // 4, b % 4]
        base = b // 4 * 4 * 33 + b * 1024
        for i in range(LIST // 2):
            code = lists_ref[b, 2 * i] + lists_ref[b, 2 * i + 1] * 32 + base
            code_of[live + i] = jnp.where(count > 2 * i + 1, code + 32768, code)
        live = live + (count + 1) // 2
    for u in range(REST):
        code_of[live + u] = 16 * 1024 + 32
    total_ref[...] = jnp.zeros_like(total_ref)
    acc[...] = jnp.zeros_like(acc)
    top[...] = jnp.full(top.shape, -jnp.inf, jnp.float32)
    mass[...] = jnp.zeros_like(mass)
    dot[...] = jnp.zeros_like(dot)

    def tiles(t):
        code = code_of[t]
        spans = [pl.ds(pl.multiple_of((code // at % 32) * BLK, BLK), BLK) for at in (1, 32)]
        return code // 1024 % 32, spans[0], spans[1], code >= 32768

    def lay(x):
        return x.reshape(-1, 8, 128)

    def scores(t):
        b, one, two, whole = tiles(t)
        kv = jnp.concatenate([window_ref[one, :], window_ref[two, :]], axis=0)
        out = lax.dot_general(kv, pairs[b], NT, preferred_element_type=jnp.float32)
        one, two = lay(out[:BLK, :BLK]) * LOG2E, lay(out[BLK:, :BLK]) * LOG2E
        other_high = jnp.where(whole, jnp.max(two, axis=0), -jnp.inf)
        old = top[b]
        high = jnp.maximum(old, jnp.maximum(jnp.max(one, axis=0), other_high))
        top[b] = high
        high_of[t] = high
        one = jnp.exp2(one - high)
        two = jnp.exp2(two - jnp.where(whole, high, jnp.inf))
        part[t, :BLK] = one.reshape(BLK, BLK)
        part[t, BLK:] = two.reshape(BLK, BLK)
        change[t] = out[:, BLK:]
        fade = jnp.exp2(old - high)
        mass[b] = mass[b] * fade + jnp.sum(one + two, axis=0)
        dot[b] = dot[b] * fade + jnp.sum(
            one * lay(out[:BLK, BLK:]) + two * lay(out[BLK:, BLK:]), axis=0
        )

    def each(step):
        many = live // UNROLL
        few = (live - many * UNROLL + REST - 1) // REST

        def run(start, count):
            def several(i, carry):
                for u in range(count):
                    step(start + i * count + u)
                return carry

            return several

        lax.fori_loop(0, many, run(0, UNROLL), 0)
        lax.fori_loop(0, few, run(many * UNROLL, REST), 0)

    each(scores)
    highest = jnp.max(top[...], axis=1, keepdims=True)
    fade = jnp.exp2(top[...] - highest)
    share = 1.0 / jnp.sum(mass[...] * fade, axis=1, keepdims=True)
    dot[...] = jnp.broadcast_to(jnp.sum(dot[...] * fade, axis=1, keepdims=True) * share, dot.shape)
    mass[...] = jnp.broadcast_to(share, mass.shape)
    top[...] = jnp.broadcast_to(highest, top.shape)

    def grads(t):
        b, one, two, _ = tiles(t)
        chance = lay(part[t]) * (jnp.exp2(high_of[t] - top[b]) * mass[b])
        grad = chance * (lay(change[t]) - dot[b])
        w = jnp.concatenate([grad.reshape(2 * BLK, BLK), chance.reshape(2 * BLK, BLK)], axis=1)
        w = w.astype(jnp.bfloat16)
        kv = jnp.concatenate([turned_ref[one, :], turned_ref[two, :]], axis=1)
        out = jnp.dot(kv, w, preferred_element_type=jnp.float32)
        acc[b, :DIM] = acc[b, :DIM] + out[:DIM, :BLK]
        acc[b, DIM:] = acc[b, DIM:] + out[DIM:, BLK:]
        out = jnp.dot(w, pairs[b], preferred_element_type=jnp.float32)
        one_sum, two_sum = total_ref[one, :] + out[:BLK], total_ref[two, :] + out[BLK:]
        total_ref[one, :] = one_sum
        total_ref[two, :] = two_sum

    each(grads)
    for b in range(16):
        out = jnp.concatenate([acc[b, :DIM] * SCALE, acc[b, DIM:]], axis=0).astype(jnp.bfloat16)
        aq_ref[b * BLK : b * BLK + BLK, :] = jnp.transpose(out)


def leave_kernel(
    aq_ref, total_ref, meta_ref,
    aq_in, kv_in,
    aq_nat, kv_nat, halo_out, halo_in, picks,
    halo_ss, halo_rs, aq_ss, aq_rs, kv_ss, kv_rs,
):
    quad, half, part, role, left, right = place()
    greet(quad, part, left, right)
    halo_out[0:8] = total_ref[0:1024, :].astype(jnp.bfloat16).reshape(8, BLK, 128)
    halo_out[8:16] = total_ref[3072:4096, :].astype(jnp.bfloat16).reshape(8, BLK, 128)

    def natural(nat, s, x):
        x = jnp.dot(picks[s], x, preferred_element_type=jnp.float32).astype(jnp.bfloat16)
        nat[pl.ds(4 * s, 4)] = x.reshape(4, BLK, 128)

    for s in range(4):
        order = jnp.concatenate([meta_ref[s, t : t + 1, :] for t in range(4)], axis=1)
        here = lax.broadcasted_iota(jnp.int32, (SEG, SEG), 0)
        picks[s] = (jnp.broadcast_to(order, (SEG, SEG)) == here).astype(jnp.bfloat16)
        natural(aq_nat, s, aq_ref[s * SEG : s * SEG + SEG, :])
    await_greetings()
    turn = [lax.rem(part // 4 + d, 4) for d in (2, 1, 3, 0)]
    for i in range(GROUP):
        there = 4 * turn[i // 4] + i % 4
        here = lax.rem(there + 8, GROUP)
        device = [jnp.where(here < 8, a, b) for a, b in zip(left, right)]
        remote(halo_out.at[here], halo_in.at[there], halo_ss.at[here], halo_rs.at[there], device).start()
        if i < len(OTHERS):
            slot = other(part, OTHERS[i])
            remote(
                aq_nat.at[slot], aq_in.at[role], aq_ss.at[slot], aq_rs.at[role], member(quad, slot)
            ).start()
    aq_in[role] = aq_nat[part]
    for s, dx in zip(turn, (2, 1, 3, 0)):
        for p in range(4):
            piece = halo_in.at[4 * s + p]
            remote(piece, piece, halo_ss.at[0], halo_rs.at[4 * s + p], left).wait_recv()
        arrived = halo_in[pl.ds(4 * s, 4)].reshape(SEG, 128).astype(jnp.float32)
        whole = total_ref[pl.ds(pl.multiple_of(1024 + s * SEG, SEG), SEG), :] + arrived
        natural(kv_nat, s, whole.astype(jnp.bfloat16))
        for dy, dc in ((1, 0), (0, 1), (1, 1), (0, 0)):
            if (dx, dy, dc) != (0, 0, 0):
                slot = other(part, (dx, dy, dc))
                remote(
                    kv_nat.at[slot], kv_in.at[role], kv_ss.at[slot], kv_rs.at[role], member(quad, slot)
                ).start()
    kv_in[role] = kv_nat[part]
    for slot in range(GROUP):
        remote(halo_out.at[slot], halo_out.at[slot], halo_ss.at[slot], halo_rs.at[0], left).wait_send()

        @pl.when(slot != part)
        def _():
            for arrived, ssem, rsem in ((aq_in, aq_ss, aq_rs), (kv_in, kv_ss, kv_rs)):
                there = arrived.at[slot]
                remote(there, there, ssem.at[slot], rsem.at[slot], left).wait_send()

        @pl.when(slot != role)
        def _():
            for arrived, ssem, rsem in ((aq_in, aq_ss, aq_rs), (kv_in, kv_ss, kv_rs)):
                there = arrived.at[slot]
                remote(there, there, ssem.at[slot], rsem.at[slot], left).wait_recv()


def finish_kernel(aq_ref, kv_ref, *refs):
    outs, made, sem = refs[:4], refs[4:8], refs[8]
    copies = []
    for i, arrived in ((0, aq_ref), (2, kv_ref)):
        for t in range(8):
            cols = slice(t * 128, t * 128 + 128)
            a, b = arrived[2 * t], arrived[2 * t + 1]
            made[i][:, cols] = jnp.concatenate([a[:, DIM:], b[:, DIM:]], axis=1)
            made[i + 1][:, cols] = jnp.concatenate([a[:, :DIM], b[:, :DIM]], axis=1)
        for j in (i, i + 1):
            copies.append(pltpu.make_async_copy(made[j], outs[j], sem.at[j]))
            copies[-1].start()
    for copy in copies:
        copy.wait()


def sems(*counts):
    return [pltpu.SemaphoreType.DMA((n,)) for n in counts]


def body(queries, keys, values, out_grad, node_order, block_lists, block_counts):
    bf, f32, i32 = jnp.bfloat16, jnp.float32, jnp.int32
    shape = jax.ShapeDtypeStruct
    slabs = pltpu.VMEM((GROUP, BLK, 128), bf)
    numbers = pltpu.VMEM((4, 16, 128), i32)
    mine = pltpu.VMEM((BLK, 16 * DIM), bf)
    window, turned, pairs, meta, lists = pl.pallas_call(
        enter_kernel,
        out_shape=[
            shape((8 * SEG, 128), bf),
            shape((8 * SEG, 128), bf),
            shape((17, 2 * BLK, 128), bf),
            shape((4, 16, 128), i32),
            shape((24, 128), i32),
        ],
        in_specs=[HBM] * 7,
        out_specs=[VMEM] * 5,
        scratch_shapes=[
            mine, mine, mine, mine,
            pltpu.VMEM((1, SEG), i32), pltpu.VMEM((4, LIST), i32), pltpu.VMEM((1, 4), i32),
            slabs, slabs, slabs, slabs, slabs, numbers, numbers, pltpu.VMEM((8, SEG, SEG), bf),
            *sems(16, 16, 16, 16, 16, 16, 4, 4, 2, 2, 7),
        ],
        compiler_params=pltpu.CompilerParams(
            collective_id=0, has_side_effects=True, vmem_limit_bytes=16 * 2**20
        ),
        name="enter",
    )(
        *(
            pltpu.with_memory_space_constraint(x, pltpu.HBM)
            for x in (
                queries, keys, values, out_grad,
                node_order.reshape(1, SEG), block_lists, block_counts.reshape(1, 4),
            )
        )
    )
    stats = pltpu.VMEM((17, 8, 128), f32)
    pairs_most = 8 * LIST + 8
    tiles = pltpu.VMEM((pairs_most, 2 * BLK, BLK), f32)
    aq, total = pl.pallas_call(
        attend_kernel,
        out_shape=[shape((4 * SEG, 128), bf), shape((8 * SEG, 128), f32)],
        in_specs=[SMEM, VMEM, VMEM, VMEM],
        out_specs=[VMEM] * 2,
        scratch_shapes=[
            pltpu.SMEM((pairs_most,), i32),
            tiles, tiles, pltpu.VMEM((pairs_most, 8, 128), f32), pltpu.VMEM((17, 128, BLK), f32),
            stats, stats, stats,
        ],
        compiler_params=pltpu.CompilerParams(vmem_limit_bytes=40 * 2**20),
        name="attend",
    )(lists, window, turned, pairs)
    aq_in, kv_in = pl.pallas_call(
        leave_kernel,
        out_shape=[shape((GROUP, BLK, 128), bf)] * 2,
        in_specs=[VMEM] * 3,
        out_specs=[VMEM] * 2,
        scratch_shapes=[
            slabs, slabs, slabs, slabs, pltpu.VMEM((4, SEG, SEG), bf),
            *sems(16, 16, 16, 16, 16, 16),
        ],
        compiler_params=pltpu.CompilerParams(
            collective_id=1, has_side_effects=True, vmem_limit_bytes=16 * 2**20
        ),
        name="leave",
    )(aq, total, meta)
    out, dq, dv, dk = pl.pallas_call(
        finish_kernel,
        out_shape=[shape((BLK, 16 * DIM), bf)] * 4,
        in_specs=[VMEM] * 2,
        out_specs=[HBM] * 4,
        scratch_shapes=[mine, mine, mine, mine, *sems(4)],
        compiler_params=pltpu.CompilerParams(vmem_limit_bytes=8 * 2**20),
        name="finish",
    )(aq_in, kv_in)
    return out, dq, dk, dv


def solution(mesh):
    rows = P(("blk", "head"), None)
    return jax.shard_map(
        body,
        mesh=mesh,
        in_specs=(rows, rows, rows, rows, P("blk"), P("blk", None), P("blk")),
        out_specs=(rows, rows, rows, rows),
        check_vma=False,
    )
```

```python
import functools
import math

import jax
import jax.numpy as jnp
from jax import lax
from jax.experimental import pallas as pl
from jax.experimental.pallas import tpu as pltpu
from jax.sharding import PartitionSpec as P

BLK = 128
SEG = 512
DIM = 64
LIST = 12
UNROLL = 40
REST = 8
GROUP = 16
NT = (((1,), (1,)), ((), ()))
TN = (((0,), (0,)), ((), ()))
SCALE = 1.0 / math.sqrt(DIM)
MESH = pl.DeviceIdType.MESH
HBM = pl.BlockSpec(memory_space=pltpu.HBM)
VMEM = pl.BlockSpec(memory_space=pltpu.VMEM)
SMEM = pl.BlockSpec(memory_space=pltpu.SMEM)


def flip(slot, half):
    return slot + half * (2 - 4 * (slot // 2 % 2))


def place():
    blk, head = lax.axis_index("blk"), lax.axis_index("head")
    quads = lax.axis_size("blk") // 4
    quad, part = blk // 4, (blk % 4) * 4 + head
    half = quad // (quads // 2)
    role = flip(part, half)
    sides = []
    for step in (quads - 1, 1):
        there = lax.rem(quad + step, quads)
        sides.append(member(there, flip(role, there // (quads // 2))))
    return quad, half, part, role, sides[0], sides[1]


def member(quad, part):
    return (quad * 4 + part // 4, part % 4)


OTHERS = [
    (2, 1, 0), (2, 0, 0), (1, 1, 0), (3, 1, 0), (2, 1, 1), (2, 0, 1), (1, 0, 0), (3, 0, 0),
    (0, 1, 0), (1, 1, 1), (3, 1, 1), (0, 1, 1), (1, 0, 1), (3, 0, 1), (0, 0, 1),
]


def other(part, steps):
    x, y, c = part // 4, part // 2 % 2, part % 2
    dx, dy, dc = steps
    x = lax.rem(x + dx, 4)
    y = 1 - y if dy else y
    c = 1 - c if dc else c
    return x * 4 + y * 2 + c


def remote(src, dst, ssem, rsem, device):
    return pltpu.make_async_remote_copy(
        src_ref=src, dst_ref=dst, send_sem=ssem, recv_sem=rsem, device_id=device, device_id_type=MESH
    )


def greet(quad, part, left, right):
    barrier = pltpu.get_barrier_semaphore()
    for steps in OTHERS:
        pl.semaphore_signal(
            barrier, inc=1, device_id=member(quad, other(part, steps)), device_id_type=MESH
        )
    for device in (left, right):
        pl.semaphore_signal(barrier, inc=1, device_id=device, device_id_type=MESH)


def await_greetings():
    pl.semaphore_wait(pltpu.get_barrier_semaphore(), GROUP + 1)


def enter_kernel(
    q_hbm, k_hbm, v_hbm, g_hbm, order_hbm, lists_hbm, counts_hbm,
    window_ref, turned_ref, pairs_ref, meta_ref, table_ref,
    q_ref, k_ref, v_ref, g_ref, order_ref, lists_ref, counts_ref,
    kv_out, qg_out, kv_in, qg_in, halo_in, meta_in, meta_halo, picks,
    kv_ss, kv_rs, qg_ss, qg_rs, halo_ss, halo_rs, meta_ss, meta_rs, side_ss, side_rs, local_sem,
):
    quad, half, part, role, left, right = place()
    seg = part // 4
    pulls = [
        pltpu.make_async_copy(src, dst, local_sem.at[i])
        for i, (src, dst) in enumerate(
            (
                (order_hbm, order_ref), (lists_hbm, lists_ref), (counts_hbm, counts_ref),
                (k_hbm, k_ref), (v_hbm, v_ref), (q_hbm, q_ref), (g_hbm, g_ref),
            )
        )
    ]
    for copy in pulls:
        copy.start()
    greet(quad, part, left, right)
    for copy in pulls[:3]:
        copy.wait()
    meta_in[seg] = jnp.zeros((16, 128), jnp.int32)
    for t in range(4):
        meta_in[seg, t : t + 1, :] = order_ref[:, t * 128 : t * 128 + 128]
    meta_in[seg, 4:8, 0:LIST] = lists_ref[...]
    meta_in[seg, 8:9, 0:4] = counts_ref[...]
    for copy in pulls[3:5]:
        copy.wait()
    for t in range(8):
        cols = slice(t * 128, t * 128 + 128)
        k, v = k_ref[:, cols], v_ref[:, cols]
        kv_out[2 * t] = jnp.concatenate([k[:, :DIM], v[:, :DIM]], axis=1)
        kv_out[2 * t + 1] = jnp.concatenate([k[:, DIM:], v[:, DIM:]], axis=1)
    await_greetings()
    sends = []

    def send(src, dst, ssem, rsem, device):
        sends.append(remote(src, dst, ssem, rsem, device))
        sends[-1].start()

    def scatter(i, out, arrived, ssem, rsem):
        there = other(part, OTHERS[i])
        send(out.at[flip(there, half)], arrived.at[part], ssem.at[i], rsem.at[part], member(quad, there))

    def landed(ref, rsem, slot):
        remote(ref.at[slot], ref.at[slot], kv_ss.at[0], rsem.at[slot], left).wait_recv()

    def pass_on(slot):
        device = [jnp.where(slot < 8, a, b) for a, b in zip(left, right)]
        there = lax.rem(slot + 8, GROUP)
        remote(kv_in.at[slot], halo_in.at[there], halo_ss.at[slot], halo_rs.at[there], device).start()

    for step in range(1, 4):
        peer = member(quad, other(part, (step, 0, 0)))
        send(meta_in.at[seg], meta_in.at[seg], meta_ss.at[step], meta_rs.at[seg], peer)
    for i in range(len(OTHERS)):
        scatter(i, kv_out, kv_in, kv_ss, kv_rs)
    kv_in[part] = kv_out[role]
    pass_on(part)
    for copy in pulls[5:]:
        copy.wait()
    for t in range(8):
        cols = slice(t * 128, t * 128 + 128)
        q, g = q_ref[:, cols] * SCALE, g_ref[:, cols]
        qg_out[2 * t] = jnp.concatenate([q[:, :DIM], g[:, :DIM]], axis=1)
        qg_out[2 * t + 1] = jnp.concatenate([q[:, DIM:], g[:, DIM:]], axis=1)
    for i in range(len(OTHERS)):
        scatter(i, qg_out, qg_in, qg_ss, qg_rs)
    qg_in[part] = qg_out[role]
    for step in range(1, 4):
        landed(meta_in, meta_rs, lax.rem(seg + step, 4))

    send(meta_in.at[0:2], meta_halo.at[2:4], side_ss.at[0], side_rs.at[1], left)
    send(meta_in.at[2:4], meta_halo.at[0:2], side_ss.at[1], side_rs.at[0], right)
    lane = lax.broadcasted_iota(jnp.int32, (SEG, 128), 1).astype(jnp.float32)

    def one_hot(at, meta):
        rows = meta[0:4].astype(jnp.float32)
        order = jnp.concatenate(
            [jnp.transpose(jnp.broadcast_to(rows[t : t + 1], (128, 128))) for t in range(4)], axis=0
        )
        for t in range(4):
            picks[at, :, t * 128 : t * 128 + 128] = (order == lane + 128.0 * t).astype(jnp.bfloat16)

    meta_ref[...] = meta_in[...]
    table_ref[...] = jnp.zeros((24, 128), jnp.int32)
    for s in range(4):
        table_ref[4 * s : 4 * s + 4, :] = meta_in[s, 4:8, :]
        table_ref[16 + s : 17 + s, :] = meta_in[s, 8:9, :]
    for dx, dy, dc in OTHERS:
        slot = other(part, (-dx % 4, dy, dc))
        landed(kv_in, kv_rs, slot)
        pass_on(slot)

    def blocked(pick, arrived, s):
        rows = arrived[4 * s : 4 * s + 4].reshape(SEG, 128)
        return jnp.dot(picks[pick], rows, preferred_element_type=jnp.float32).astype(jnp.bfloat16)

    def keep(at, kv):
        window_ref[at : at + SEG, :] = kv
        for i in range(0, SEG, BLK):
            turned_ref[at + i : at + i + BLK, :] = jnp.transpose(kv[i : i + BLK])

    for s in range(4):
        one_hot(s, meta_in[s])
    for side in range(2):
        two = meta_halo.at[2 * side : 2 * side + 2]
        remote(two, two, side_ss.at[side], side_rs.at[side], left).wait_recv()
        for s in (2 * side, 2 * side + 1):
            one_hot(4 + s, meta_halo[s])
    for s in range(4):
        keep(1024 + s * SEG, blocked(s, kv_in, s))
    for dx, dy, dc in OTHERS:
        landed(qg_in, qg_rs, other(part, (-dx % 4, dy, dc)))
    low = lax.broadcasted_iota(jnp.int32, (SEG, 128), 1) < DIM
    for s in range(4):
        qg = blocked(s, qg_in, s)
        zero = jnp.zeros_like(qg)
        pairs_ref[4 * s : 4 * s + 4, :BLK] = jnp.where(low, qg, zero).reshape(4, BLK, 128)
        pairs_ref[4 * s : 4 * s + 4, BLK:] = jnp.where(low, zero, qg).reshape(4, BLK, 128)
    for slot in range(GROUP):
        landed(halo_in, halo_rs, slot)
    for s in range(4):
        keep((s if s < 2 else s + 4) * SEG, blocked(4 + s, halo_in, s))
    pairs_ref[16] = jnp.zeros((2 * BLK, 128), jnp.bfloat16)
    for copy in sends:
        copy.wait_send()
    for slot in range(GROUP):
        remote(kv_in.at[slot], kv_in.at[slot], halo_ss.at[slot], halo_rs.at[slot], left).wait_send()


def attend_kernel(
    lists_ref, window_ref, turned_ref, pairs, aq_ref, total_ref,
    code_of, part, change, high_of, acc, top, mass, dot,
):
    live = 0
    for b in range(16):
        count = lists_ref[16 + b // 4, b % 4]
        base = b // 4 * 4 * 33 + b * 1024
        for i in range(LIST // 2):
            code = lists_ref[b, 2 * i] + lists_ref[b, 2 * i + 1] * 32 + base
            code_of[live + i] = jnp.where(count > 2 * i + 1, code + 32768, code)
        live = live + (count + 1) // 2
    for u in range(REST):
        code_of[live + u] = 16 * 1024 + 32
    total_ref[...] = jnp.zeros_like(total_ref)
    acc[...] = jnp.zeros_like(acc)
    top[...] = jnp.full(top.shape, -jnp.inf, jnp.float32)
    mass[...] = jnp.zeros_like(mass)
    dot[...] = jnp.zeros_like(dot)

    def tiles(t):
        code = code_of[t]
        spans = [pl.ds(pl.multiple_of(((code >> at) & 31) * BLK, BLK), BLK) for at in (0, 5)]
        return (code >> 10) & 31, spans[0], spans[1], code >= 32768

    def lay(x):
        return x.reshape(-1, 8, 128)

    def scores(t):
        b, one, two, whole = tiles(t)
        kv = jnp.concatenate([window_ref[one, :], window_ref[two, :]], axis=0)
        out = lax.dot_general(kv, pairs[b], NT, preferred_element_type=jnp.float32)
        one, two = lay(out[:BLK, :BLK]), lay(out[BLK:, :BLK])
        other_high = jnp.where(whole, jnp.max(two, axis=0), -jnp.inf)
        old = top[b]
        high = jnp.maximum(old, jnp.maximum(jnp.max(one, axis=0), other_high))
        top[b] = high
        high_of[t] = high
        one = jnp.exp(one - high)
        two = jnp.exp(two - jnp.where(whole, high, jnp.inf))
        part[t, :BLK] = one.reshape(BLK, BLK)
        part[t, BLK:] = two.reshape(BLK, BLK)
        change[t] = out[:, BLK:]
        fade = jnp.exp(old - high)
        mass[b] = mass[b] * fade + jnp.sum(one + two, axis=0)
        dot[b] = dot[b] * fade + jnp.sum(
            one * lay(out[:BLK, BLK:]) + two * lay(out[BLK:, BLK:]), axis=0
        )

    def each(step):
        many = live // UNROLL
        few = (live - many * UNROLL + REST - 1) // REST

        def run(start, count):
            def several(i, carry):
                for u in range(count):
                    step(start + i * count + u)
                return carry

            return several

        lax.fori_loop(0, many, run(0, UNROLL), 0)
        lax.fori_loop(0, few, run(many * UNROLL, REST), 0)

    each(scores)
    highest = jnp.max(top[...], axis=1, keepdims=True)
    fade = jnp.exp(top[...] - highest)
    share = 1.0 / jnp.sum(mass[...] * fade, axis=1, keepdims=True)
    dot[...] = jnp.broadcast_to(jnp.sum(dot[...] * fade, axis=1, keepdims=True) * share, dot.shape)
    mass[...] = jnp.broadcast_to(share, mass.shape)
    top[...] = jnp.broadcast_to(highest, top.shape)

    def grads(t):
        b, one, two, _ = tiles(t)
        chance = lay(part[t]) * (jnp.exp(high_of[t] - top[b]) * mass[b])
        grad = chance * (lay(change[t]) - dot[b])
        w = jnp.concatenate([grad.reshape(2 * BLK, BLK), chance.reshape(2 * BLK, BLK)], axis=1)
        w = w.astype(jnp.bfloat16)
        kv = jnp.concatenate([turned_ref[one, :], turned_ref[two, :]], axis=1)
        out = jnp.dot(kv, w, preferred_element_type=jnp.float32)
        acc[b, :DIM] = acc[b, :DIM] + out[:DIM, :BLK]
        acc[b, DIM:] = acc[b, DIM:] + out[DIM:, BLK:]
        out = jnp.dot(w, pairs[b], preferred_element_type=jnp.float32)
        one_sum, two_sum = total_ref[one, :] + out[:BLK], total_ref[two, :] + out[BLK:]
        total_ref[one, :] = one_sum
        total_ref[two, :] = two_sum

    each(grads)
    for b in range(16):
        out = jnp.concatenate([acc[b, :DIM] * SCALE, acc[b, DIM:]], axis=0).astype(jnp.bfloat16)
        aq_ref[b * BLK : b * BLK + BLK, :] = jnp.transpose(out)


def leave_kernel(
    aq_ref, total_ref, meta_ref,
    aq_in, kv_in,
    aq_nat, kv_nat, halo_out, halo_in, picks,
    halo_ss, halo_rs, aq_ss, aq_rs, kv_ss, kv_rs,
):
    quad, half, part, role, left, right = place()
    greet(quad, part, left, right)
    halo_out[0:8] = total_ref[0:1024, :].astype(jnp.bfloat16).reshape(8, BLK, 128)
    halo_out[8:16] = total_ref[3072:4096, :].astype(jnp.bfloat16).reshape(8, BLK, 128)

    def natural(nat, s, x):
        x = jnp.dot(picks[s], x, preferred_element_type=jnp.float32).astype(jnp.bfloat16)
        nat[pl.ds(4 * s, 4)] = x.reshape(4, BLK, 128)

    for s in range(4):
        order = jnp.concatenate([meta_ref[s, t : t + 1, :] for t in range(4)], axis=1)
        here = lax.broadcasted_iota(jnp.int32, (SEG, SEG), 0)
        picks[s] = (jnp.broadcast_to(order, (SEG, SEG)) == here).astype(jnp.bfloat16)
        natural(aq_nat, s, aq_ref[s * SEG : s * SEG + SEG, :])
    await_greetings()
    turn = [lax.rem(part // 4 + d, 4) for d in (2, 1, 3, 0)]
    for i in range(GROUP):
        there = 4 * turn[i // 4] + i % 4
        here = lax.rem(there + 8, GROUP)
        device = [jnp.where(here < 8, a, b) for a, b in zip(left, right)]
        remote(halo_out.at[here], halo_in.at[there], halo_ss.at[here], halo_rs.at[there], device).start()
    for steps in OTHERS:
        slot = other(part, steps)
        remote(
            aq_nat.at[slot], aq_in.at[role], aq_ss.at[slot], aq_rs.at[role], member(quad, slot)
        ).start()
    aq_in[role] = aq_nat[part]
    for s, dx in zip(turn, (2, 1, 3, 0)):
        for p in range(4):
            piece = halo_in.at[4 * s + p]
            remote(piece, piece, halo_ss.at[0], halo_rs.at[4 * s + p], left).wait_recv()
        arrived = halo_in[pl.ds(4 * s, 4)].reshape(SEG, 128).astype(jnp.float32)
        whole = total_ref[pl.ds(pl.multiple_of(1024 + s * SEG, SEG), SEG), :] + arrived
        natural(kv_nat, s, whole.astype(jnp.bfloat16))
        for dy, dc in ((1, 0), (0, 1), (1, 1), (0, 0)):
            if (dx, dy, dc) != (0, 0, 0):
                slot = other(part, (dx, dy, dc))
                remote(
                    kv_nat.at[slot], kv_in.at[role], kv_ss.at[slot], kv_rs.at[role], member(quad, slot)
                ).start()
    kv_in[role] = kv_nat[part]
    for slot in range(GROUP):
        remote(halo_out.at[slot], halo_out.at[slot], halo_ss.at[slot], halo_rs.at[0], left).wait_send()

        @pl.when(slot != part)
        def _():
            for arrived, ssem, rsem in ((aq_in, aq_ss, aq_rs), (kv_in, kv_ss, kv_rs)):
                there = arrived.at[slot]
                remote(there, there, ssem.at[slot], rsem.at[slot], left).wait_send()

        @pl.when(slot != role)
        def _():
            for arrived, ssem, rsem in ((aq_in, aq_ss, aq_rs), (kv_in, kv_ss, kv_rs)):
                there = arrived.at[slot]
                remote(there, there, ssem.at[slot], rsem.at[slot], left).wait_recv()


def finish_kernel(aq_ref, kv_ref, *refs):
    outs, made, sem = refs[:4], refs[4:8], refs[8]
    copies = []
    for i, arrived in ((0, aq_ref), (2, kv_ref)):
        for t in range(8):
            cols = slice(t * 128, t * 128 + 128)
            a, b = arrived[2 * t], arrived[2 * t + 1]
            made[i][:, cols] = jnp.concatenate([a[:, DIM:], b[:, DIM:]], axis=1)
            made[i + 1][:, cols] = jnp.concatenate([a[:, :DIM], b[:, :DIM]], axis=1)
        for j in (i, i + 1):
            copies.append(pltpu.make_async_copy(made[j], outs[j], sem.at[j]))
            copies[-1].start()
    for copy in copies:
        copy.wait()


def sems(*counts):
    return [pltpu.SemaphoreType.DMA((n,)) for n in counts]


def body(queries, keys, values, out_grad, node_order, block_lists, block_counts):
    bf, f32, i32 = jnp.bfloat16, jnp.float32, jnp.int32
    shape = jax.ShapeDtypeStruct
    slabs = pltpu.VMEM((GROUP, BLK, 128), bf)
    numbers = pltpu.VMEM((4, 16, 128), i32)
    mine = pltpu.VMEM((BLK, 16 * DIM), bf)
    window, turned, pairs, meta, lists = pl.pallas_call(
        enter_kernel,
        out_shape=[
            shape((8 * SEG, 128), bf),
            shape((8 * SEG, 128), bf),
            shape((17, 2 * BLK, 128), bf),
            shape((4, 16, 128), i32),
            shape((24, 128), i32),
        ],
        in_specs=[HBM] * 7,
        out_specs=[VMEM] * 5,
        scratch_shapes=[
            mine, mine, mine, mine,
            pltpu.VMEM((1, SEG), i32), pltpu.VMEM((4, LIST), i32), pltpu.VMEM((1, 4), i32),
            slabs, slabs, slabs, slabs, slabs, numbers, numbers, pltpu.VMEM((8, SEG, SEG), bf),
            *sems(16, 16, 16, 16, 16, 16, 4, 4, 2, 2, 7),
        ],
        compiler_params=pltpu.CompilerParams(
            collective_id=0, has_side_effects=True, vmem_limit_bytes=16 * 2**20
        ),
        name="enter",
    )(
        *(
            pltpu.with_memory_space_constraint(x, pltpu.HBM)
            for x in (
                queries, keys, values, out_grad,
                node_order.reshape(1, SEG), block_lists, block_counts.reshape(1, 4),
            )
        )
    )
    stats = pltpu.VMEM((17, 8, 128), f32)
    pairs_most = 8 * LIST + 8
    tiles = pltpu.VMEM((pairs_most, 2 * BLK, BLK), f32)
    aq, total = pl.pallas_call(
        attend_kernel,
        out_shape=[shape((4 * SEG, 128), bf), shape((8 * SEG, 128), f32)],
        in_specs=[SMEM, VMEM, VMEM, VMEM],
        out_specs=[VMEM] * 2,
        scratch_shapes=[
            pltpu.SMEM((pairs_most,), i32),
            tiles, tiles, pltpu.VMEM((pairs_most, 8, 128), f32), pltpu.VMEM((17, 128, BLK), f32),
            stats, stats, stats,
        ],
        compiler_params=pltpu.CompilerParams(vmem_limit_bytes=40 * 2**20),
        name="attend",
    )(lists, window, turned, pairs)
    aq_in, kv_in = pl.pallas_call(
        leave_kernel,
        out_shape=[shape((GROUP, BLK, 128), bf)] * 2,
        in_specs=[VMEM] * 3,
        out_specs=[VMEM] * 2,
        scratch_shapes=[
            slabs, slabs, slabs, slabs, pltpu.VMEM((4, SEG, SEG), bf),
            *sems(16, 16, 16, 16, 16, 16),
        ],
        compiler_params=pltpu.CompilerParams(
            collective_id=1, has_side_effects=True, vmem_limit_bytes=16 * 2**20
        ),
        name="leave",
    )(aq, total, meta)
    out, dq, dv, dk = pl.pallas_call(
        finish_kernel,
        out_shape=[shape((BLK, 16 * DIM), bf)] * 4,
        in_specs=[VMEM] * 2,
        out_specs=[HBM] * 4,
        scratch_shapes=[mine, mine, mine, mine, *sems(4)],
        compiler_params=pltpu.CompilerParams(vmem_limit_bytes=8 * 2**20),
        name="finish",
    )(aq_in, kv_in)
    return out, dq, dk, dv


def solution(mesh):
    rows = P(("blk", "head"), None)
    return jax.shard_map(
        body,
        mesh=mesh,
        in_specs=(rows, rows, rows, rows, P("blk"), P("blk", None), P("blk")),
        out_specs=(rows, rows, rows, rows),
        check_vma=False,
    )
```

```python
import functools
import math

import jax
import jax.numpy as jnp
from jax import lax
from jax.experimental import pallas as pl
from jax.experimental.pallas import tpu as pltpu
from jax.sharding import PartitionSpec as P

BLK = 128
SEG = 512
DIM = 64
LIST = 12
UNROLL = 40
MIDDLE = 16
REST = 8
GROUP = 16
NT = (((1,), (1,)), ((), ()))
TN = (((0,), (0,)), ((), ()))
SCALE = 1.0 / math.sqrt(DIM)
MESH = pl.DeviceIdType.MESH
HBM = pl.BlockSpec(memory_space=pltpu.HBM)
VMEM = pl.BlockSpec(memory_space=pltpu.VMEM)
SMEM = pl.BlockSpec(memory_space=pltpu.SMEM)


def flip(slot, half):
    return slot + half * (2 - 4 * (slot // 2 % 2))


def place():
    blk, head = lax.axis_index("blk"), lax.axis_index("head")
    quads = lax.axis_size("blk") // 4
    quad, part = blk // 4, (blk % 4) * 4 + head
    half = quad // (quads // 2)
    role = flip(part, half)
    sides = []
    for step in (quads - 1, 1):
        there = lax.rem(quad + step, quads)
        sides.append(member(there, flip(role, there // (quads // 2))))
    return quad, half, part, role, sides[0], sides[1]


def member(quad, part):
    return (quad * 4 + part // 4, part % 4)


OTHERS = [
    (2, 1, 0), (2, 0, 0), (1, 1, 0), (3, 1, 0), (2, 1, 1), (2, 0, 1), (1, 0, 0), (3, 0, 0),
    (0, 1, 0), (1, 1, 1), (3, 1, 1), (0, 1, 1), (1, 0, 1), (3, 0, 1), (0, 0, 1),
]


def other(part, steps):
    x, y, c = part // 4, part // 2 % 2, part % 2
    dx, dy, dc = steps
    x = lax.rem(x + dx, 4)
    y = 1 - y if dy else y
    c = 1 - c if dc else c
    return x * 4 + y * 2 + c


def remote(src, dst, ssem, rsem, device):
    return pltpu.make_async_remote_copy(
        src_ref=src, dst_ref=dst, send_sem=ssem, recv_sem=rsem, device_id=device, device_id_type=MESH
    )


def greet(quad, part, left, right):
    barrier = pltpu.get_barrier_semaphore()
    for steps in OTHERS:
        pl.semaphore_signal(
            barrier, inc=1, device_id=member(quad, other(part, steps)), device_id_type=MESH
        )
    for device in (left, right):
        pl.semaphore_signal(barrier, inc=1, device_id=device, device_id_type=MESH)


def await_greetings():
    pl.semaphore_wait(pltpu.get_barrier_semaphore(), GROUP + 1)


def enter_kernel(
    q_hbm, k_hbm, v_hbm, g_hbm, order_hbm, lists_hbm, counts_hbm,
    window_ref, turned_ref, pairs_ref, meta_ref, table_ref,
    q_ref, k_ref, v_ref, g_ref, order_ref, lists_ref, counts_ref,
    kv_out, qg_out, kv_in, qg_in, halo_in, meta_in, meta_halo, picks,
    kv_ss, kv_rs, qg_ss, qg_rs, halo_ss, halo_rs, meta_ss, meta_rs, side_ss, side_rs, local_sem,
):
    quad, half, part, role, left, right = place()
    seg = part // 4
    pulls = [
        pltpu.make_async_copy(src, dst, local_sem.at[i])
        for i, (src, dst) in enumerate(
            (
                (order_hbm, order_ref), (lists_hbm, lists_ref), (counts_hbm, counts_ref),
                (k_hbm, k_ref), (v_hbm, v_ref), (q_hbm, q_ref), (g_hbm, g_ref),
            )
        )
    ]
    for copy in pulls:
        copy.start()
    greet(quad, part, left, right)
    for copy in pulls[:3]:
        copy.wait()
    meta_in[seg] = jnp.zeros((16, 128), jnp.int32)
    for t in range(4):
        meta_in[seg, t : t + 1, :] = order_ref[:, t * 128 : t * 128 + 128]
    meta_in[seg, 4:8, 0:LIST] = lists_ref[...]
    meta_in[seg, 8:9, 0:4] = counts_ref[...]
    for copy in pulls[3:5]:
        copy.wait()
    for t in range(8):
        cols = slice(t * 128, t * 128 + 128)
        k, v = k_ref[:, cols], v_ref[:, cols]
        kv_out[2 * t] = jnp.concatenate([k[:, :DIM], v[:, :DIM]], axis=1)
        kv_out[2 * t + 1] = jnp.concatenate([k[:, DIM:], v[:, DIM:]], axis=1)
    await_greetings()
    sends = []

    def send(src, dst, ssem, rsem, device):
        sends.append(remote(src, dst, ssem, rsem, device))
        sends[-1].start()

    def scatter(i, out, arrived, ssem, rsem):
        there = other(part, OTHERS[i])
        send(out.at[flip(there, half)], arrived.at[part], ssem.at[i], rsem.at[part], member(quad, there))

    def landed(ref, rsem, slot):
        remote(ref.at[slot], ref.at[slot], kv_ss.at[0], rsem.at[slot], left).wait_recv()

    def pass_on(slot):
        device = [jnp.where(slot < 8, a, b) for a, b in zip(left, right)]
        there = lax.rem(slot + 8, GROUP)
        remote(kv_in.at[slot], halo_in.at[there], halo_ss.at[slot], halo_rs.at[there], device).start()

    for step in range(1, 4):
        peer = member(quad, other(part, (step, 0, 0)))
        send(meta_in.at[seg], meta_in.at[seg], meta_ss.at[step], meta_rs.at[seg], peer)
    for i in range(len(OTHERS)):
        scatter(i, kv_out, kv_in, kv_ss, kv_rs)
    kv_in[part] = kv_out[role]
    pass_on(part)
    for copy in pulls[5:]:
        copy.wait()
    for t in range(8):
        cols = slice(t * 128, t * 128 + 128)
        q, g = q_ref[:, cols] * SCALE, g_ref[:, cols]
        qg_out[2 * t] = jnp.concatenate([q[:, :DIM], g[:, :DIM]], axis=1)
        qg_out[2 * t + 1] = jnp.concatenate([q[:, DIM:], g[:, DIM:]], axis=1)
    for i in range(len(OTHERS)):
        scatter(i, qg_out, qg_in, qg_ss, qg_rs)
    qg_in[part] = qg_out[role]
    for step in range(1, 4):
        landed(meta_in, meta_rs, lax.rem(seg + step, 4))

    send(meta_in.at[0:2], meta_halo.at[2:4], side_ss.at[0], side_rs.at[1], left)
    send(meta_in.at[2:4], meta_halo.at[0:2], side_ss.at[1], side_rs.at[0], right)
    lane = lax.broadcasted_iota(jnp.int32, (SEG, 128), 1).astype(jnp.float32)

    def one_hot(at, meta):
        rows = meta[0:4].astype(jnp.float32)
        order = jnp.concatenate(
            [jnp.transpose(jnp.broadcast_to(rows[t : t + 1], (128, 128))) for t in range(4)], axis=0
        )
        for t in range(4):
            picks[at, :, t * 128 : t * 128 + 128] = (order == lane + 128.0 * t).astype(jnp.bfloat16)

    meta_ref[...] = meta_in[...]
    table_ref[...] = jnp.zeros((24, 128), jnp.int32)
    for s in range(4):
        table_ref[4 * s : 4 * s + 4, :] = meta_in[s, 4:8, :]
        table_ref[16 + s : 17 + s, :] = meta_in[s, 8:9, :]
    for dx, dy, dc in OTHERS:
        slot = other(part, (-dx % 4, dy, dc))
        landed(kv_in, kv_rs, slot)
        pass_on(slot)

    def blocked(pick, arrived, s):
        rows = arrived[4 * s : 4 * s + 4].reshape(SEG, 128)
        return jnp.dot(picks[pick], rows, preferred_element_type=jnp.float32).astype(jnp.bfloat16)

    def keep(at, kv):
        window_ref[at : at + SEG, :] = kv
        for i in range(0, SEG, BLK):
            turned_ref[at + i : at + i + BLK, :] = jnp.transpose(kv[i : i + BLK])

    for s in range(4):
        one_hot(s, meta_in[s])
    for side in range(2):
        two = meta_halo.at[2 * side : 2 * side + 2]
        remote(two, two, side_ss.at[side], side_rs.at[side], left).wait_recv()
        for s in (2 * side, 2 * side + 1):
            one_hot(4 + s, meta_halo[s])
    for s in range(4):
        keep(1024 + s * SEG, blocked(s, kv_in, s))
    for dx, dy, dc in OTHERS:
        landed(qg_in, qg_rs, other(part, (-dx % 4, dy, dc)))
    low = lax.broadcasted_iota(jnp.int32, (SEG, 128), 1) < DIM
    for s in range(4):
        qg = blocked(s, qg_in, s)
        zero = jnp.zeros_like(qg)
        pairs_ref[4 * s : 4 * s + 4, :BLK] = jnp.where(low, qg, zero).reshape(4, BLK, 128)
        pairs_ref[4 * s : 4 * s + 4, BLK:] = jnp.where(low, zero, qg).reshape(4, BLK, 128)
    for slot in range(GROUP):
        landed(halo_in, halo_rs, slot)
    for s in range(4):
        keep((s if s < 2 else s + 4) * SEG, blocked(4 + s, halo_in, s))
    pairs_ref[16] = jnp.zeros((2 * BLK, 128), jnp.bfloat16)
    for copy in sends:
        copy.wait_send()
    for slot in range(GROUP):
        remote(kv_in.at[slot], kv_in.at[slot], halo_ss.at[slot], halo_rs.at[slot], left).wait_send()


def attend_kernel(
    lists_ref, window_ref, turned_ref, pairs, aq_ref, total_ref,
    code_of, part, change, high_of, acc, top, mass, dot,
):
    live = 0
    for b in range(16):
        count = lists_ref[16 + b // 4, b % 4]
        base = b // 4 * 4 * 33 + b * 1024
        for i in range(LIST // 2):
            code = lists_ref[b, 2 * i] + lists_ref[b, 2 * i + 1] * 32 + base
            code_of[live + i] = jnp.where(count > 2 * i + 1, code + 32768, code)
        live = live + (count + 1) // 2
    for u in range(REST):
        code_of[live + u] = 16 * 1024 + 32
    total_ref[...] = jnp.zeros_like(total_ref)
    acc[...] = jnp.zeros_like(acc)
    top[...] = jnp.full(top.shape, -jnp.inf, jnp.float32)
    mass[...] = jnp.zeros_like(mass)
    dot[...] = jnp.zeros_like(dot)

    def tiles(t):
        code = code_of[t]
        spans = [pl.ds(pl.multiple_of(((code >> at) & 31) * BLK, BLK), BLK) for at in (0, 5)]
        return (code >> 10) & 31, spans[0], spans[1], code >= 32768

    def lay(x):
        return x.reshape(-1, 8, 128)

    def scores(t):
        b, one, two, whole = tiles(t)
        kv = jnp.concatenate([window_ref[one, :], window_ref[two, :]], axis=0)
        out = lax.dot_general(kv, pairs[b], NT, preferred_element_type=jnp.float32)
        one, two = lay(out[:BLK, :BLK]), lay(out[BLK:, :BLK])
        other_high = jnp.where(whole, jnp.max(two, axis=0), -jnp.inf)
        old = top[b]
        high = jnp.maximum(old, jnp.maximum(jnp.max(one, axis=0), other_high))
        top[b] = high
        high_of[t] = high
        one = jnp.exp(one - high)
        two = jnp.exp(two - jnp.where(whole, high, jnp.inf))
        part[t, :BLK] = one.reshape(BLK, BLK)
        part[t, BLK:] = two.reshape(BLK, BLK)
        change[t] = out[:, BLK:]
        fade = jnp.exp(old - high)
        mass[b] = mass[b] * fade + jnp.sum(one + two, axis=0)
        dot[b] = dot[b] * fade + jnp.sum(
            one * lay(out[:BLK, BLK:]) + two * lay(out[BLK:, BLK:]), axis=0
        )

    def each(step):
        many = live // UNROLL
        some = (live - many * UNROLL) // MIDDLE
        done = many * UNROLL + some * MIDDLE
        few = (live - done + REST - 1) // REST

        def run(start, count):
            def several(i, carry):
                for u in range(count):
                    step(start + i * count + u)
                return carry

            return several

        lax.fori_loop(0, many, run(0, UNROLL), 0)
        lax.fori_loop(0, some, run(many * UNROLL, MIDDLE), 0)
        lax.fori_loop(0, few, run(done, REST), 0)

    each(scores)
    highest = jnp.max(top[...], axis=1, keepdims=True)
    fade = jnp.exp(top[...] - highest)
    share = 1.0 / jnp.sum(mass[...] * fade, axis=1, keepdims=True)
    dot[...] = jnp.broadcast_to(jnp.sum(dot[...] * fade, axis=1, keepdims=True) * share, dot.shape)
    mass[...] = jnp.broadcast_to(share, mass.shape)
    top[...] = jnp.broadcast_to(highest, top.shape)

    def grads(t):
        b, one, two, _ = tiles(t)
        chance = lay(part[t]) * (jnp.exp(high_of[t] - top[b]) * mass[b])
        grad = chance * (lay(change[t]) - dot[b])
        w = jnp.concatenate([grad.reshape(2 * BLK, BLK), chance.reshape(2 * BLK, BLK)], axis=1)
        w = w.astype(jnp.bfloat16)
        kv = jnp.concatenate([turned_ref[one, :], turned_ref[two, :]], axis=1)
        out = jnp.dot(kv, w, preferred_element_type=jnp.float32)
        acc[b, :DIM] = acc[b, :DIM] + out[:DIM, :BLK]
        acc[b, DIM:] = acc[b, DIM:] + out[DIM:, BLK:]
        out = jnp.dot(w, pairs[b], preferred_element_type=jnp.float32)
        one_sum, two_sum = total_ref[one, :] + out[:BLK], total_ref[two, :] + out[BLK:]
        total_ref[one, :] = one_sum
        total_ref[two, :] = two_sum

    each(grads)
    for b in range(16):
        out = jnp.concatenate([acc[b, :DIM] * SCALE, acc[b, DIM:]], axis=0).astype(jnp.bfloat16)
        aq_ref[b * BLK : b * BLK + BLK, :] = jnp.transpose(out)


def leave_kernel(
    aq_ref, total_ref, meta_ref,
    aq_in, kv_in,
    aq_nat, kv_nat, halo_out, halo_in, picks,
    halo_ss, halo_rs, aq_ss, aq_rs, kv_ss, kv_rs,
):
    quad, half, part, role, left, right = place()
    greet(quad, part, left, right)
    halo_out[0:8] = total_ref[0:1024, :].astype(jnp.bfloat16).reshape(8, BLK, 128)
    halo_out[8:16] = total_ref[3072:4096, :].astype(jnp.bfloat16).reshape(8, BLK, 128)

    def natural(nat, s, x):
        x = jnp.dot(picks[s], x, preferred_element_type=jnp.float32).astype(jnp.bfloat16)
        nat[pl.ds(4 * s, 4)] = x.reshape(4, BLK, 128)

    for s in range(4):
        order = jnp.concatenate([meta_ref[s, t : t + 1, :] for t in range(4)], axis=1)
        here = lax.broadcasted_iota(jnp.int32, (SEG, SEG), 0)
        picks[s] = (jnp.broadcast_to(order, (SEG, SEG)) == here).astype(jnp.bfloat16)
        natural(aq_nat, s, aq_ref[s * SEG : s * SEG + SEG, :])
    await_greetings()
    turn = [lax.rem(part // 4 + d, 4) for d in (2, 1, 3, 0)]
    for i in range(GROUP):
        there = 4 * turn[i // 4] + i % 4
        here = lax.rem(there + 8, GROUP)
        device = [jnp.where(here < 8, a, b) for a, b in zip(left, right)]
        remote(halo_out.at[here], halo_in.at[there], halo_ss.at[here], halo_rs.at[there], device).start()
    for steps in OTHERS:
        slot = other(part, steps)
        remote(
            aq_nat.at[slot], aq_in.at[role], aq_ss.at[slot], aq_rs.at[role], member(quad, slot)
        ).start()
    aq_in[role] = aq_nat[part]
    for s, dx in zip(turn, (2, 1, 3, 0)):
        for p in range(4):
            piece = halo_in.at[4 * s + p]
            remote(piece, piece, halo_ss.at[0], halo_rs.at[4 * s + p], left).wait_recv()
        arrived = halo_in[pl.ds(4 * s, 4)].reshape(SEG, 128).astype(jnp.float32)
        whole = total_ref[pl.ds(pl.multiple_of(1024 + s * SEG, SEG), SEG), :] + arrived
        natural(kv_nat, s, whole.astype(jnp.bfloat16))
        for dy, dc in ((1, 0), (0, 1), (1, 1), (0, 0)):
            if (dx, dy, dc) != (0, 0, 0):
                slot = other(part, (dx, dy, dc))
                remote(
                    kv_nat.at[slot], kv_in.at[role], kv_ss.at[slot], kv_rs.at[role], member(quad, slot)
                ).start()
    kv_in[role] = kv_nat[part]
    for slot in range(GROUP):
        remote(halo_out.at[slot], halo_out.at[slot], halo_ss.at[slot], halo_rs.at[0], left).wait_send()

        @pl.when(slot != part)
        def _():
            for arrived, ssem, rsem in ((aq_in, aq_ss, aq_rs), (kv_in, kv_ss, kv_rs)):
                there = arrived.at[slot]
                remote(there, there, ssem.at[slot], rsem.at[slot], left).wait_send()

        @pl.when(slot != role)
        def _():
            for arrived, ssem, rsem in ((aq_in, aq_ss, aq_rs), (kv_in, kv_ss, kv_rs)):
                there = arrived.at[slot]
                remote(there, there, ssem.at[slot], rsem.at[slot], left).wait_recv()


def finish_kernel(aq_ref, kv_ref, *refs):
    outs, made, sem = refs[:4], refs[4:8], refs[8]
    copies = []
    for i, arrived in ((0, aq_ref), (2, kv_ref)):
        for t in range(8):
            cols = slice(t * 128, t * 128 + 128)
            a, b = arrived[2 * t], arrived[2 * t + 1]
            made[i][:, cols] = jnp.concatenate([a[:, DIM:], b[:, DIM:]], axis=1)
            made[i + 1][:, cols] = jnp.concatenate([a[:, :DIM], b[:, :DIM]], axis=1)
        for j in (i, i + 1):
            copies.append(pltpu.make_async_copy(made[j], outs[j], sem.at[j]))
            copies[-1].start()
    for copy in copies:
        copy.wait()


def sems(*counts):
    return [pltpu.SemaphoreType.DMA((n,)) for n in counts]


def body(queries, keys, values, out_grad, node_order, block_lists, block_counts):
    bf, f32, i32 = jnp.bfloat16, jnp.float32, jnp.int32
    shape = jax.ShapeDtypeStruct
    slabs = pltpu.VMEM((GROUP, BLK, 128), bf)
    numbers = pltpu.VMEM((4, 16, 128), i32)
    mine = pltpu.VMEM((BLK, 16 * DIM), bf)
    window, turned, pairs, meta, lists = pl.pallas_call(
        enter_kernel,
        out_shape=[
            shape((8 * SEG, 128), bf),
            shape((8 * SEG, 128), bf),
            shape((17, 2 * BLK, 128), bf),
            shape((4, 16, 128), i32),
            shape((24, 128), i32),
        ],
        in_specs=[HBM] * 7,
        out_specs=[VMEM] * 5,
        scratch_shapes=[
            mine, mine, mine, mine,
            pltpu.VMEM((1, SEG), i32), pltpu.VMEM((4, LIST), i32), pltpu.VMEM((1, 4), i32),
            slabs, slabs, slabs, slabs, slabs, numbers, numbers, pltpu.VMEM((8, SEG, SEG), bf),
            *sems(16, 16, 16, 16, 16, 16, 4, 4, 2, 2, 7),
        ],
        compiler_params=pltpu.CompilerParams(
            collective_id=0, has_side_effects=True, vmem_limit_bytes=16 * 2**20
        ),
        name="enter",
    )(
        *(
            pltpu.with_memory_space_constraint(x, pltpu.HBM)
            for x in (
                queries, keys, values, out_grad,
                node_order.reshape(1, SEG), block_lists, block_counts.reshape(1, 4),
            )
        )
    )
    stats = pltpu.VMEM((17, 8, 128), f32)
    pairs_most = 8 * LIST + 8
    tiles = pltpu.VMEM((pairs_most, 2 * BLK, BLK), f32)
    aq, total = pl.pallas_call(
        attend_kernel,
        out_shape=[shape((4 * SEG, 128), bf), shape((8 * SEG, 128), f32)],
        in_specs=[SMEM, VMEM, VMEM, VMEM],
        out_specs=[VMEM] * 2,
        scratch_shapes=[
            pltpu.SMEM((pairs_most,), i32),
            tiles, tiles, pltpu.VMEM((pairs_most, 8, 128), f32), pltpu.VMEM((17, 128, BLK), f32),
            stats, stats, stats,
        ],
        compiler_params=pltpu.CompilerParams(vmem_limit_bytes=40 * 2**20),
        name="attend",
    )(lists, window, turned, pairs)
    aq_in, kv_in = pl.pallas_call(
        leave_kernel,
        out_shape=[shape((GROUP, BLK, 128), bf)] * 2,
        in_specs=[VMEM] * 3,
        out_specs=[VMEM] * 2,
        scratch_shapes=[
            slabs, slabs, slabs, slabs, pltpu.VMEM((4, SEG, SEG), bf),
            *sems(16, 16, 16, 16, 16, 16),
        ],
        compiler_params=pltpu.CompilerParams(
            collective_id=1, has_side_effects=True, vmem_limit_bytes=16 * 2**20
        ),
        name="leave",
    )(aq, total, meta)
    out, dq, dv, dk = pl.pallas_call(
        finish_kernel,
        out_shape=[shape((BLK, 16 * DIM), bf)] * 4,
        in_specs=[VMEM] * 2,
        out_specs=[HBM] * 4,
        scratch_shapes=[mine, mine, mine, mine, *sems(4)],
        compiler_params=pltpu.CompilerParams(vmem_limit_bytes=8 * 2**20),
        name="finish",
    )(aq_in, kv_in)
    return out, dq, dk, dv


def solution(mesh):
    rows = P(("blk", "head"), None)
    return jax.shard_map(
        body,
        mesh=mesh,
        in_specs=(rows, rows, rows, rows, P("blk"), P("blk", None), P("blk")),
        out_specs=(rows, rows, rows, rows),
        check_vma=False,
    )
```
